256 devices in a mesh: row: 32 (over z, y), col: 8 (over x, core).
Axes of the slice: x: 4, y: 4, z: 8, core: 2. Of those that a mesh axis runs over, the one named last changes fastest.
Arguments:
- candidates: float32 [1024, 131072], P('col', 'row'), may hold values from -64 to 64
- trailing: float32 [512, 131072], P('col', 'row'), may hold values from -64 to 64
- pivots: int32 [64], replicated, may hold values from 0 to 1023, as said below
Outputs:
- r_panel: float32 [64, 64], replicated
- r_trail: float32 [64, 512], P(None, 'col')
- basis: float32 [64, 131072], P(None, 'row')
- trailing_next: float32 [512, 131072], P('col', 'row')
The draws below stay inside these ranges and needn't reach their ends.
Inputs may be any that keep to these rules, and one draw needn't show every extreme that they name: `pivots`: 64 distinct column numbers; one block of 128 consecutive columns (those of one index of col) holds exactly 32 of them and no block holds more.
All inputs are finite; a program needn't handle non-finite values.
Results may differ from the reference program's by a relative error of at most 0.0003.
Values sent between devices are 32-bit elements; how exact they have to be, the bound alone decides.
No kernel may reach another device: no remote copies, remote signals or barrier semaphores. Data moves between devices by JAX's collectives and lax.ppermute only.
A program may use at most 64 MiB of HBM per device.

```python
import jax
import jax.numpy as jnp
from jax import lax

ROWS_DEV = 4096
CAND_DEV = 128
K = 64
TRAIL = 512
ROWS = 131072
N_ROW = 32
N_COL = 8


def drawn_all(key):
    rows_all = ROWS_DEV * N_ROW
    cand_all = CAND_DEV * N_COL
    keys = [jax.random.fold_in(key, 7100 + i) for i in range(12)]
    heavy = jax.random.randint(keys[0], (), 0, N_COL)
    own_cols = jax.random.permutation(keys[1], CAND_DEV)[:K // 2] + heavy * CAND_DEV
    spread = jax.random.permutation(keys[2], (N_COL - 1) * CAND_DEV)[:K - K // 2]
    spread_dev = spread // CAND_DEV
    spread_dev = spread_dev + (spread_dev >= heavy).astype(jnp.int32)
    other_cols = spread_dev * CAND_DEV + spread % CAND_DEV
    chosen = jnp.concatenate([own_cols.astype(jnp.int32), other_cols.astype(jnp.int32)])
    chosen = chosen[jax.random.permutation(keys[3], K)].astype(jnp.int32)
    noise = jax.random.truncated_normal(keys[4], -6.0, 6.0, (cand_all, rows_all), jnp.float32)
    ramp = jnp.arange(rows_all, dtype=jnp.float32) / jnp.float32(rows_all - 1)
    rise = jnp.exp(jnp.log(3.0) * ramp)
    row_scale = jnp.exp(jax.random.uniform(keys[5], (rows_all,), jnp.float32, jnp.log(0.3), jnp.log(3.0)))
    col_scale = jnp.exp(jax.random.uniform(keys[6], (cand_all,), jnp.float32, jnp.log(0.3), jnp.log(3.0)))
    base = noise
    cands = jnp.clip(base * (row_scale * rise)[None, :] * col_scale[:, None], -64.0, 64.0)
    panel = jnp.take(cands, chosen, axis=0)
    mixing = jax.random.truncated_normal(keys[9], -3.0, 3.0, (TRAIL, K), jnp.float32)
    extra = jax.random.truncated_normal(keys[10], -6.0, 6.0, (TRAIL, rows_all), jnp.float32)
    mixed = jnp.dot(mixing, panel, preferred_element_type=jnp.float32, precision=lax.Precision.HIGHEST)
    trail = jnp.clip(extra + mixed / jnp.sqrt(jnp.float32(K)), -64.0, 64.0)
    return (cands, trail, chosen)


def draw_candidates(key, part):
    return drawn_all(key)[0]


def draw_trailing(key, part):
    return drawn_all(key)[1]


def draw_pivots(key, part):
    return drawn_all(key)[2]


def setup_inputs(seed: int = 0) -> dict:
    splits = jax.random.split(jax.random.key(seed), 4)
    candidates = draw_candidates(jax.random.fold_in(splits[3], 71), 0)
    trailing = draw_trailing(jax.random.fold_in(splits[3], 71), 0)
    pivots = draw_pivots(jax.random.fold_in(splits[3], 71), 0)
    return dict(candidates=candidates, trailing=trailing, pivots=pivots)


def reference(candidates, trailing, pivots):
    panel = jnp.take(candidates, pivots, axis=0)
    gram = jnp.dot(panel.astype(jnp.float32), panel.T.astype(jnp.float32), preferred_element_type=jnp.float32, precision=lax.Precision.HIGHEST)
    upper = jnp.linalg.cholesky(gram).T
    ortho = jax.scipy.linalg.solve_triangular(upper, panel, trans=1, lower=False)
    projected = jnp.dot(ortho.astype(jnp.float32), trailing.T.astype(jnp.float32), preferred_element_type=jnp.float32, precision=lax.Precision.HIGHEST)
    trailing_next = trailing - jnp.dot(projected.T.astype(jnp.float32), ortho.astype(jnp.float32), preferred_element_type=jnp.float32, precision=lax.Precision.HIGHEST)
    root_rows = jnp.sqrt(jnp.float32(ROWS))
    return (upper / root_rows, projected / root_rows, ortho * root_rows, trailing_next)
```

```python
import functools

import jax
import jax.numpy as jnp
import numpy as np
from jax import lax
from jax.experimental import pallas as pl
from jax.experimental.pallas import tpu as pltpu
from jax.sharding import PartitionSpec as P

VMEM = pltpu.VMEM
SMEM = pltpu.SMEM
CORES = 2


def split_bf16(value):
    high = value.astype(jnp.bfloat16)
    low = (value - high.astype(jnp.float32)).astype(jnp.bfloat16)
    return high, low


def select_kernel(capacity, x_count, where_ref, pivots_ref, cand_ref, *rest):
    outs, (rows, sems) = rest[:x_count], rest[x_count:]
    cand_count, width = cand_ref.shape
    count = pivots_ref.shape[0]
    me = where_ref[0] * CORES + where_ref[1]

    def row_copy(pivot, slot):
        return pltpu.make_async_copy(
            cand_ref.at[pl.ds(pivot - me * cand_count, 1), :], rows.at[pl.ds(slot, 1), :], sems.at[slot]
        )

    def fetch(i, slot):
        pivot = pivots_ref[i]
        mine = pivot // cand_count == me

        @pl.when(mine)
        def _():
            row_copy(pivot, slot).start()

        return slot + mine.astype(jnp.int32)

    total = lax.fori_loop(0, count, fetch, jnp.int32(0))

    def drain(slot, carry):
        row_copy(me * cand_count, slot).wait()
        return carry

    lax.fori_loop(0, total, drain, 0)
    part = width // x_count
    for k in range(x_count):
        begin = pl.multiple_of((where_ref[0] ^ k) * part, part)
        outs[k][...] = rows[:, pl.ds(begin, part)]


def merge_kernel(x_count, where_ref, owners_ref, slots_ref, *rest):
    sources, (keep_ref, send_ref) = rest[:x_count], rest[x_count:]
    count, half = keep_ref.shape
    my_x, my_core = where_ref[0], where_ref[1]
    keep_at = pl.multiple_of(my_core * half, half)
    send_at = pl.multiple_of((1 - my_core) * half, half)

    def place(i, carry):
        owner = owners_ref[i]
        slot = slots_ref[i]
        away = (owner // CORES) ^ my_x

        for k in range(x_count):

            @pl.when((owner % CORES == my_core) & (away == k))
            def _():
                keep_ref[pl.ds(i, 1), :] = sources[k][pl.ds(slot, 1), pl.ds(keep_at, half)]
                send_ref[pl.ds(i, 1), :] = sources[k][pl.ds(slot, 1), pl.ds(send_at, half)]

        return carry

    lax.fori_loop(0, count, place, 0)


def gram_kernel(x_count, where_ref, *rest):
    mine, other = rest[:x_count], rest[x_count : 2 * x_count]
    trail_ref, sums_ref, panel_ref = rest[2 * x_count :]
    count, piece = mine[0].shape
    width = trail_ref.shape[1]
    my_x, my_core = where_ref[0], where_ref[1]
    for k in range(x_count):
        for core, ref in ((my_core, mine[k]), (1 - my_core, other[k])):
            begin = pl.multiple_of(((my_x ^ k) * CORES + core) * piece, piece)
            high, low = split_bf16(ref[...])
            panel_ref[0:count, pl.ds(begin, piece)] = high
            panel_ref[count : 2 * count, pl.ds(begin, piece)] = low
    total = jnp.zeros((2 * count, 4 * count), jnp.float32)
    for begin in range(0, width, piece):
        block = slice(begin, begin + piece)
        trail_high, trail_low = split_bf16(trail_ref[:, block])
        panel_parts = panel_ref[:, block]
        right = jnp.concatenate(
            [panel_parts[:count], trail_high, panel_parts[count:], trail_low], axis=0
        )
        total += lax.dot_general(
            panel_parts, right, (((1,), (1,)), ((), ())), preferred_element_type=jnp.float32
        )
    lead = total[:count] + total[count:]
    sums_ref[...] = lead[:, : 2 * count] + lead[:, 2 * count :]


def eliminate(work):
    count = work.shape[0]
    rows = lax.broadcasted_iota(jnp.int32, work.shape, 0)
    lanes = lax.broadcasted_iota(jnp.int32, work.shape, 1)
    scale = jnp.zeros(work.shape, jnp.float32)
    for j in range(count):
        row = jnp.broadcast_to(work[j : j + 1, :], work.shape)
        column = jnp.broadcast_to(work[:, j : j + 1], work.shape)
        pivot = jnp.broadcast_to(column[j : j + 1, :], work.shape)
        scale = jnp.where(rows == j, lax.rsqrt(pivot), scale)
        factor = jnp.where(rows > j, column / pivot, 0.0)
        here = lanes == j
        work = jnp.where(here & (rows > j), 0.0, work) - factor * jnp.where(here, 1.0, row)
    return work * scale, scale


def finish_kernel(root, one_ref, two_ref, panel_ref, trail_ref, upper_ref, coef_ref, basis_ref, next_ref, left):
    count = one_ref.shape[0]

    @pl.when(pl.program_id(0) == 0)
    def _():
        work, scale = eliminate(one_ref[...] + two_ref[...])
        square = (count, count)
        rows = lax.broadcasted_iota(jnp.int32, square, 0)
        lanes = lax.broadcasted_iota(jnp.int32, square, 1)
        factor, coef = work[:, :count], work[:, count:]
        upper_ref[...] = jnp.where(lanes >= rows, factor, 0.0) * jnp.float32(1.0 / root)
        coef_ref[...] = coef * jnp.float32(1.0 / root)
        inverse = jnp.where(lanes < rows, factor, jnp.where(lanes == rows, scale[:, :count], 0.0))
        weights = lax.dot_general(
            coef,
            inverse,
            (((0,), (0,)), ((), ())),
            preferred_element_type=jnp.float32,
            precision=lax.Precision.HIGHEST,
        )
        high, low = split_bf16(jnp.concatenate([inverse * jnp.float32(root), weights], axis=0))
        left[...] = jnp.concatenate([high, high, low, low], axis=1)

    block = panel_ref[...]
    both = jnp.dot(
        left[...], jnp.concatenate([block, block], axis=0), preferred_element_type=jnp.float32
    )
    basis_ref[...] = both[:count]
    next_ref[...] = trail_ref[...] - both[count:]


def on_device(candidates, trailing, pivots):
    cand_count, width = candidates.shape
    count = pivots.shape[0]
    col_count, row_count = lax.axis_size("col"), lax.axis_size("row")
    x_count = col_count // CORES
    capacity = count // 2
    piece = width // col_count
    root = float(np.sqrt(np.float32(width * row_count)))
    my_col = lax.axis_index("col")
    place = jnp.stack([my_col // CORES, my_col % CORES]).astype(jnp.int32)
    owners = pivots // cand_count
    order = jnp.arange(count, dtype=jnp.int32)
    earlier = (owners[:, None] == owners[None, :]) & (order[None, :] < order[:, None])
    slots = jnp.sum(earlier.astype(jnp.int32), axis=1)
    f32 = jnp.float32

    def to_x(array, k):
        return lax.ppermute(
            array, "col", [(i, ((i // CORES) ^ k) * CORES + i % CORES) for i in range(col_count)]
        )

    def to_core(array):
        return lax.ppermute(array, "col", [(i, i ^ 1) for i in range(col_count)])

    def to_row(array, k):
        return lax.ppermute(array, "row", [(i, i ^ k) for i in range(row_count)])

    in_vmem, in_smem = pl.BlockSpec(memory_space=VMEM), pl.BlockSpec(memory_space=SMEM)
    quarters = pl.pallas_call(
        functools.partial(select_kernel, capacity, x_count),
        out_shape=[jax.ShapeDtypeStruct((capacity, width // x_count), f32)] * x_count,
        in_specs=[in_smem, in_smem, pl.BlockSpec(memory_space=pl.ANY)],
        out_specs=[in_vmem] * x_count,
        scratch_shapes=[VMEM((capacity, width), f32), pltpu.SemaphoreType.DMA((capacity,))],
        name="select",
    )(place, pivots, candidates)
    arrived = [quarters[0]] + [to_x(quarters[k], k) for k in range(1, x_count)]
    keep, send = pl.pallas_call(
        functools.partial(merge_kernel, x_count),
        out_shape=[jax.ShapeDtypeStruct((count, piece), f32)] * 2,
        in_specs=[in_smem] * 3 + [in_vmem] * x_count,
        out_specs=[in_vmem] * 2,
        name="merge",
    )(place, owners, slots, *arrived)
    passed = to_core(send)
    own_core = (owners % CORES == my_col % CORES)[:, None]
    own_piece = jnp.where(own_core, keep, passed)
    mine = [own_piece] + [to_x(own_piece, k) for k in range(1, x_count)]
    other = [to_core(array) for array in mine]
    sums, panel = pl.pallas_call(
        functools.partial(gram_kernel, x_count),
        out_shape=[
            jax.ShapeDtypeStruct((count, 2 * count), f32),
            jax.ShapeDtypeStruct((2 * count, width), jnp.bfloat16),
        ],
        in_specs=[in_smem] + [in_vmem] * (2 * x_count + 1),
        out_specs=[in_vmem] * 2,
        name="gram",
    )(place, *mine, *other, trailing)
    sums = (sums + to_row(sums, 1)) + (to_row(sums, 2) + to_row(sums, 3))
    sums = (sums + to_row(sums, 4)) + (to_row(sums, 8) + to_row(sums, 12))
    far = to_row(sums, 16)
    steps = col_count
    whole = lambda shape: pl.BlockSpec(shape, lambda i: (0, 0))
    block = lambda rows: pl.BlockSpec((rows, width // steps), lambda i: (0, i))
    return pl.pallas_call(
        functools.partial(finish_kernel, root),
        grid=(steps,),
        out_shape=[
            jax.ShapeDtypeStruct((count, count), f32),
            jax.ShapeDtypeStruct((count, count), f32),
            jax.ShapeDtypeStruct((count, width), f32),
            jax.ShapeDtypeStruct((count, width), f32),
        ],
        in_specs=[whole((count, 2 * count))] * 2 + [block(2 * count), block(count)],
        out_specs=[whole((count, count))] * 2 + [block(count)] * 2,
        scratch_shapes=[VMEM((2 * count, 4 * count), jnp.bfloat16)],
        name="finish",
    )(sums, far, panel, trailing)


def solution(mesh):
    placed = (P("col", "row"), P("col", "row"), P())
    return jax.shard_map(
        on_device,
        mesh=mesh,
        in_specs=placed,
        out_specs=(P(), P(None, "col"), P(None, "row"), P("col", "row")),
        check_vma=False,
    )
```

```python
import functools

import jax
import jax.numpy as jnp
import numpy as np
from jax import lax
from jax.experimental import pallas as pl
from jax.experimental.pallas import tpu as pltpu
from jax.sharding import PartitionSpec as P

VMEM = pltpu.VMEM
SMEM = pltpu.SMEM
CORES = 2


def split_bf16(value):
    high = value.astype(jnp.bfloat16)
    low = (value - high.astype(jnp.float32)).astype(jnp.bfloat16)
    return high, low


def select_kernel(x_count, pivots_ref, cand_ref, *rest):
    outs, (rows, sems) = rest[:x_count], rest[x_count:]
    cand_count, width = cand_ref.shape
    count = pivots_ref.shape[0]
    me = lax.axis_index("col")
    rows[...] = jnp.zeros_like(rows)

    def row_copy(pivot, slot):
        return pltpu.make_async_copy(
            cand_ref.at[pl.ds(pivot - me * cand_count, 1), :], rows.at[pl.ds(slot, 1), :], sems.at[slot]
        )

    def fetch(i, slot):
        pivot = pivots_ref[i]
        mine = pivot // cand_count == me

        @pl.when(mine)
        def _():
            row_copy(pivot, slot).start()

        return slot + mine.astype(jnp.int32)

    total = lax.fori_loop(0, count, fetch, jnp.int32(0))

    def drain(slot, carry):
        row_copy(me * cand_count, slot).wait()
        return carry

    lax.fori_loop(0, total, drain, 0)
    part = width // x_count
    for k in range(x_count):
        begin = pl.multiple_of(((me // CORES) ^ k) * part, part)
        outs[k][...] = rows[:, pl.ds(begin, part)]


def merge_kernel(x_count, keys_ref, *rest):
    sources, (keep_ref, send_ref) = rest[:x_count], rest[x_count:]
    count, half = keep_ref.shape
    held = x_count * sources[0].shape[0]
    my_core = lax.axis_index("col") % CORES
    lanes = lax.broadcasted_iota(jnp.int32, (count, held), 1)
    pick = (keys_ref[...] == lanes).astype(jnp.float32).astype(jnp.bfloat16)
    pick = jnp.concatenate([pick, pick], axis=1)
    for out_ref, core in ((send_ref, 1 - my_core), (keep_ref, my_core)):
        begin = pl.multiple_of(core * half, half)
        value = jnp.concatenate([ref[:, pl.ds(begin, half)] for ref in sources], axis=0)
        parts = jnp.concatenate(split_bf16(value), axis=0)
        out_ref[...] = jnp.dot(pick, parts, preferred_element_type=jnp.float32)


def gram_kernel(x_count, *rest):
    mine, other = rest[:x_count], rest[x_count : 2 * x_count]
    trail_ref, sums_ref, panel_ref = rest[2 * x_count :]
    count, piece = mine[0].shape
    width = trail_ref.shape[1]
    me = lax.axis_index("col")
    my_x, my_core = me // CORES, me % CORES
    for k in range(x_count):
        for core, ref in ((my_core, mine[k]), (1 - my_core, other[k])):
            begin = pl.multiple_of(((my_x ^ k) * CORES + core) * piece, piece)
            high, low = split_bf16(ref[...])
            panel_ref[0:count, pl.ds(begin, piece)] = high
            panel_ref[count : 2 * count, pl.ds(begin, piece)] = low
    total = jnp.zeros((2 * count, 4 * count), jnp.float32)
    for begin in range(0, width, piece):
        block = slice(begin, begin + piece)
        trail_high, trail_low = split_bf16(trail_ref[:, block])
        panel_parts = panel_ref[:, block]
        right = jnp.concatenate(
            [panel_parts[:count], trail_high, panel_parts[count:], trail_low], axis=0
        )
        total += lax.dot_general(
            panel_parts, right, (((1,), (1,)), ((), ())), preferred_element_type=jnp.float32
        )
    lead = total[:count] + total[count:]
    sums_ref[...] = lead[:, : 2 * count] + lead[:, 2 * count :]


def eliminate(work):
    count = work.shape[0]
    rows = lax.broadcasted_iota(jnp.int32, work.shape, 0)
    lanes = lax.broadcasted_iota(jnp.int32, work.shape, 1)
    scale = jnp.zeros(work.shape, jnp.float32)
    for j in range(count):
        row = jnp.broadcast_to(work[j : j + 1, :], work.shape)
        column = jnp.broadcast_to(work[:, j : j + 1], work.shape)
        pivot = jnp.broadcast_to(column[j : j + 1, :], work.shape)
        scale = jnp.where(rows == j, lax.rsqrt(pivot), scale)
        factor = jnp.where(rows > j, column / pivot, 0.0)
        here = lanes == j
        work = jnp.where(here & (rows > j), 0.0, work) - factor * jnp.where(here, 1.0, row)
    return work * scale, scale


def finish_kernel(root, one_ref, two_ref, panel_ref, trail_ref, upper_ref, coef_ref, basis_ref, next_ref, left):
    count = one_ref.shape[0]

    @pl.when(pl.program_id(0) == 0)
    def _():
        work, scale = eliminate(one_ref[...] + two_ref[...])
        square = (count, count)
        rows = lax.broadcasted_iota(jnp.int32, square, 0)
        lanes = lax.broadcasted_iota(jnp.int32, square, 1)
        factor, coef = work[:, :count], work[:, count:]
        upper_ref[...] = jnp.where(lanes >= rows, factor, 0.0) * jnp.float32(1.0 / root)
        coef_ref[...] = coef * jnp.float32(1.0 / root)
        inverse = jnp.where(lanes < rows, factor, jnp.where(lanes == rows, scale[:, :count], 0.0))
        weights = lax.dot_general(
            coef,
            inverse,
            (((0,), (0,)), ((), ())),
            preferred_element_type=jnp.float32,
            precision=lax.Precision.HIGHEST,
        )
        high, low = split_bf16(jnp.concatenate([inverse * jnp.float32(root), weights], axis=0))
        left[...] = jnp.concatenate([high, high, low, low], axis=1)

    width = next_ref.shape[1]
    here = pl.ds(pl.multiple_of(pl.program_id(0) * width, width), width)
    block = panel_ref[:, here]
    both = jnp.dot(
        left[...], jnp.concatenate([block, block], axis=0), preferred_element_type=jnp.float32
    )
    basis_ref[...] = both[:count]
    next_ref[...] = trail_ref[...] - both[count:]


def on_device(candidates, trailing, pivots):
    cand_count, width = candidates.shape
    count = pivots.shape[0]
    col_count, row_count = lax.axis_size("col"), lax.axis_size("row")
    x_count = col_count // CORES
    capacity = count // 2
    piece = width // col_count
    root = float(np.sqrt(np.float32(width * row_count)))
    my_col = lax.axis_index("col")
    owners = pivots // cand_count
    order = jnp.arange(count, dtype=jnp.int32)
    earlier = (owners[:, None] == owners[None, :]) & (order[None, :] < order[:, None])
    slots = jnp.sum(earlier.astype(jnp.int32), axis=1)
    away = (owners // CORES) ^ (my_col // CORES)
    keys = jnp.where(owners % CORES == my_col % CORES, away * capacity + slots, -1)[:, None]
    f32 = jnp.float32

    def to_x(array, k):
        return lax.ppermute(
            array, "col", [(i, ((i // CORES) ^ k) * CORES + i % CORES) for i in range(col_count)]
        )

    def to_core(array):
        return lax.ppermute(array, "col", [(i, i ^ 1) for i in range(col_count)])

    def to_row(array, k):
        return lax.ppermute(array, "row", [(i, i ^ k) for i in range(row_count)])

    def near(array):
        return pltpu.with_memory_space_constraint(array, VMEM)

    in_vmem, in_smem = pl.BlockSpec(memory_space=VMEM), pl.BlockSpec(memory_space=SMEM)
    quarters = pl.pallas_call(
        functools.partial(select_kernel, x_count),
        out_shape=[VMEM((capacity, width // x_count), f32)] * x_count,
        in_specs=[in_smem, pl.BlockSpec(memory_space=pl.ANY)],
        out_specs=[in_vmem] * x_count,
        scratch_shapes=[VMEM((capacity, width), f32), pltpu.SemaphoreType.DMA((capacity,))],
        name="select",
    )(pivots, candidates)
    arrived = [quarters[0]] + [to_x(quarters[k], k) for k in range(1, x_count)]
    keep, send = pl.pallas_call(
        functools.partial(merge_kernel, x_count),
        out_shape=[VMEM((count, piece), f32)] * 2,
        in_specs=[in_vmem] * (1 + x_count),
        out_specs=[in_vmem] * 2,
        name="merge",
    )(near(keys), *map(near, arrived))
    own_piece = keep + to_core(send)
    mine = [own_piece] + [to_x(own_piece, k) for k in range(1, x_count)]
    other = [to_core(array) for array in mine]
    sums, panel = pl.pallas_call(
        functools.partial(gram_kernel, x_count),
        out_shape=[VMEM((count, 2 * count), f32), VMEM((2 * count, width), jnp.bfloat16)],
        in_specs=[in_vmem] * (2 * x_count + 1),
        out_specs=[in_vmem] * 2,
        name="gram",
    )(*map(near, mine), *map(near, other), near(trailing))
    step = 1
    while step < row_count // 2:
        sums = sums + to_row(sums, step)
        step *= 2
    far = to_row(sums, step)
    steps = col_count
    whole = lambda shape: pl.BlockSpec(shape, lambda i: (0, 0))
    block = lambda rows: pl.BlockSpec((rows, width // steps), lambda i: (0, i))
    return pl.pallas_call(
        functools.partial(finish_kernel, root),
        grid=(steps,),
        out_shape=[
            jax.ShapeDtypeStruct((count, count), f32),
            jax.ShapeDtypeStruct((count, count), f32),
            jax.ShapeDtypeStruct((count, width), f32),
            jax.ShapeDtypeStruct((count, width), f32),
        ],
        in_specs=[in_vmem] * 3 + [block(count)],
        out_specs=[whole((count, count))] * 2 + [block(count)] * 2,
        scratch_shapes=[VMEM((2 * count, 4 * count), jnp.bfloat16)],
        name="finish",
    )(near(sums), near(far), near(panel), trailing)


def solution(mesh):
    placed = (P("col", "row"), P("col", "row"), P())
    return jax.shard_map(
        on_device,
        mesh=mesh,
        in_specs=placed,
        out_specs=(P(), P(None, "col"), P(None, "row"), P("col", "row")),
        check_vma=False,
    )
```

```python
import functools

import jax
import jax.numpy as jnp
import numpy as np
from jax import lax
from jax.experimental import pallas as pl
from jax.experimental.pallas import tpu as pltpu
from jax.sharding import PartitionSpec as P

VMEM = pltpu.VMEM
SMEM = pltpu.SMEM
CORES = 2


def split_bf16(value):
    high = value.astype(jnp.bfloat16)
    low = (value - high.astype(jnp.float32)).astype(jnp.bfloat16)
    return high, low


def select_kernel(x_count, pivots_ref, cand_ref, *rest):
    outs, (rows, sems) = rest[:x_count], rest[x_count:]
    cand_count, width = cand_ref.shape
    count = pivots_ref.shape[0]
    me = lax.axis_index("col")
    rows[...] = jnp.zeros_like(rows)

    def row_copy(pivot, slot):
        return pltpu.make_async_copy(
            cand_ref.at[pl.ds(pivot - me * cand_count, 1), :], rows.at[pl.ds(slot, 1), :], sems.at[slot]
        )

    def fetch(i, slot):
        pivot = pivots_ref[i]
        mine = pivot // cand_count == me

        @pl.when(mine)
        def _():
            row_copy(pivot, slot).start()

        return slot + mine.astype(jnp.int32)

    total = lax.fori_loop(0, count, fetch, jnp.int32(0), unroll=8)

    def drain(slot, carry):
        row_copy(me * cand_count, slot).wait()
        return carry

    lax.fori_loop(0, total, drain, 0)
    part = width // x_count
    for k in range(x_count):
        begin = pl.multiple_of(((me // CORES) ^ k) * part, part)
        outs[k][...] = rows[:, pl.ds(begin, part)]


def merge_kernel(x_count, keys_ref, *rest):
    sources, (keep_ref, send_ref) = rest[:x_count], rest[x_count:]
    count, half = keep_ref.shape
    held = x_count * sources[0].shape[0]
    my_core = lax.axis_index("col") % CORES
    lanes = lax.broadcasted_iota(jnp.int32, (count, held), 1)
    pick = (keys_ref[...] == lanes).astype(jnp.float32).astype(jnp.bfloat16)
    pick = jnp.concatenate([pick, pick], axis=1)
    for out_ref, core in ((send_ref, 1 - my_core), (keep_ref, my_core)):
        begin = pl.multiple_of(core * half, half)
        value = jnp.concatenate([ref[:, pl.ds(begin, half)] for ref in sources], axis=0)
        parts = jnp.concatenate(split_bf16(value), axis=0)
        out_ref[...] = jnp.dot(pick, parts, preferred_element_type=jnp.float32)


def gram_kernel(x_count, *rest):
    mine, other = rest[:x_count], rest[x_count : 2 * x_count]
    trail_ref, sums_ref, panel_ref = rest[2 * x_count :]
    count, piece = mine[0].shape
    width = trail_ref.shape[1]
    me = lax.axis_index("col")
    my_x, my_core = me // CORES, me % CORES
    for k in range(x_count):
        for core, ref in ((my_core, mine[k]), (1 - my_core, other[k])):
            begin = pl.multiple_of(((my_x ^ k) * CORES + core) * piece, piece)
            high, low = split_bf16(ref[...])
            panel_ref[0:count, pl.ds(begin, piece)] = high
            panel_ref[count : 2 * count, pl.ds(begin, piece)] = low
    total = jnp.zeros((2 * count, 4 * count), jnp.float32)
    for begin in range(0, width, piece):
        block = slice(begin, begin + piece)
        trail_high, trail_low = split_bf16(trail_ref[:, block])
        panel_parts = panel_ref[:, block]
        right = jnp.concatenate(
            [panel_parts[:count], trail_high, panel_parts[count:], trail_low], axis=0
        )
        total += lax.dot_general(
            panel_parts, right, (((1,), (1,)), ((), ())), preferred_element_type=jnp.float32
        )
    lead = total[:count] + total[count:]
    sums_ref[...] = lead[:, : 2 * count] + lead[:, 2 * count :]


def outer_sum(left, right):
    def parts(value):
        first = value.astype(jnp.bfloat16).astype(jnp.float32)
        rest = value - first
        second = rest.astype(jnp.bfloat16).astype(jnp.float32)
        return first, second, rest - second

    l1, l2, l3 = parts(left)
    r1, r2, r3 = parts(right)
    return lax.dot_general(
        jnp.concatenate([l1, l1, l2, l2, l1, l3], axis=0).astype(jnp.bfloat16),
        jnp.concatenate([r1, r2, r1, r2, r3, r1], axis=0).astype(jnp.bfloat16),
        (((0,), (0,)), ((), ())),
        preferred_element_type=jnp.float32,
    )


def eliminate(work):
    size = 8
    count, width = work.shape
    shape = (size, width)
    blocks = [work[begin : begin + size] for begin in range(0, count, size)]
    rows = lax.broadcasted_iota(jnp.int32, shape, 0)
    lanes = lax.broadcasted_iota(jnp.int32, shape, 1)
    scales = []
    for b in range(len(blocks)):
        block = blocks[b]
        columns = [
            jnp.broadcast_to(block[:, size * b + k : size * b + k + 1], shape) for k in range(size)
        ]
        scale = jnp.zeros(shape, jnp.float32)
        for j in range(size):
            pivot = jnp.broadcast_to(columns[j][j : j + 1], shape)
            scale = jnp.where(rows == j, lax.rsqrt(pivot), scale)
            below = rows > j
            factor = jnp.where(below, columns[j] * (1.0 / pivot), 0.0)
            for k in range(j + 1, size):
                columns[k] -= factor * jnp.broadcast_to(columns[k][j : j + 1], shape)
            here = lanes == size * b + j
            row = jnp.where(here, 1.0, jnp.broadcast_to(block[j : j + 1], shape))
            block = jnp.where(here & below, 0.0, block) - factor * row
        block *= scale
        blocks[b] = block
        scales.append(scale)
        if b + 1 < len(blocks):
            place = lanes - size * b
            inside = (place >= 0) & (place < size)
            inverse = jnp.where(place < rows, block, jnp.where(place == rows, scale, 0.0))
            update = outer_sum(block[:, :count], jnp.where(inside, inverse, block))
            for c in range(b + 1, len(blocks)):
                blocks[c] = jnp.where(inside, 0.0, blocks[c]) - update[size * c : size * (c + 1)]
    return jnp.concatenate(blocks, axis=0), jnp.concatenate(scales, axis=0)


def finish_kernel(
    root, one_ref, two_ref, panel_ref, trail_ref, upper_ref, coef_ref, basis_ref, next_ref, trail, basis, left_over, in_sem, out_sems
):
    count = one_ref.shape[0]
    fetch = pltpu.make_async_copy(trail_ref, trail, in_sem)
    fetch.start()
    work, scale = eliminate(one_ref[...] + two_ref[...])
    square = (count, count)
    rows = lax.broadcasted_iota(jnp.int32, square, 0)
    lanes = lax.broadcasted_iota(jnp.int32, square, 1)
    factor, coef = work[:, :count], work[:, count:]
    upper_ref[...] = jnp.where(lanes >= rows, factor, 0.0) * jnp.float32(1.0 / root)
    coef_ref[...] = coef * jnp.float32(1.0 / root)
    inverse = jnp.where(lanes < rows, factor, jnp.where(lanes == rows, scale[:, :count], 0.0))
    weights = outer_sum(coef, inverse)
    high, low = split_bf16(jnp.concatenate([inverse * jnp.float32(root), weights], axis=0))
    left = jnp.concatenate([high, high, low, low], axis=1)
    fetch.wait()
    chunks = out_sems.shape[0]
    width = panel_ref.shape[1] // chunks
    copies = []
    for c in range(chunks):
        here = slice(c * width, (c + 1) * width)
        block = panel_ref[:, here]
        both = jnp.dot(
            left, jnp.concatenate([block, block], axis=0), preferred_element_type=jnp.float32
        )
        basis[:, here] = both[:count]
        left_over[:, here] = trail[:, here] - both[count:]
        for i, (source, target) in enumerate(((basis, basis_ref), (left_over, next_ref))):
            copy = pltpu.make_async_copy(source.at[:, here], target.at[:, here], out_sems.at[c, i])
            copy.start()
            copies.append(copy)
    for copy in copies:
        copy.wait()


def on_device(candidates, trailing, pivots):
    cand_count, width = candidates.shape
    count = pivots.shape[0]
    col_count, row_count = lax.axis_size("col"), lax.axis_size("row")
    x_count = col_count // CORES
    capacity = count // 2
    piece = width // col_count
    root = float(np.sqrt(np.float32(width * row_count)))
    my_col = lax.axis_index("col")
    owners = pivots // cand_count
    order = jnp.arange(count, dtype=jnp.int32)
    earlier = (owners[:, None] == owners[None, :]) & (order[None, :] < order[:, None])
    slots = jnp.sum(earlier.astype(jnp.int32), axis=1)
    away = (owners // CORES) ^ (my_col // CORES)
    keys = jnp.where(owners % CORES == my_col % CORES, away * capacity + slots, -1)[:, None]
    f32 = jnp.float32

    def to_x(array, k):
        return lax.ppermute(
            array, "col", [(i, ((i // CORES) ^ k) * CORES + i % CORES) for i in range(col_count)]
        )

    def to_core(array):
        return lax.ppermute(array, "col", [(i, i ^ 1) for i in range(col_count)])

    def to_row(array, k):
        return lax.ppermute(array, "row", [(i, i ^ k) for i in range(row_count)])

    def near(array):
        return pltpu.with_memory_space_constraint(array, VMEM)

    in_vmem, in_smem = pl.BlockSpec(memory_space=VMEM), pl.BlockSpec(memory_space=SMEM)
    quarters = pl.pallas_call(
        functools.partial(select_kernel, x_count),
        out_shape=[VMEM((capacity, width // x_count), f32)] * x_count,
        in_specs=[in_smem, pl.BlockSpec(memory_space=pl.ANY)],
        out_specs=[in_vmem] * x_count,
        scratch_shapes=[VMEM((capacity, width), f32), pltpu.SemaphoreType.DMA((capacity,))],
        name="select",
    )(pivots, candidates)
    arrived = [quarters[0]] + [to_x(quarters[k], k) for k in range(1, x_count)]
    keep, send = pl.pallas_call(
        functools.partial(merge_kernel, x_count),
        out_shape=[VMEM((count, piece), f32)] * 2,
        in_specs=[in_vmem] * (1 + x_count),
        out_specs=[in_vmem] * 2,
        name="merge",
    )(near(keys), *map(near, arrived))
    own_piece = keep + to_core(send)
    mine = [own_piece] + [to_x(own_piece, k) for k in range(1, x_count)]
    other = [to_core(array) for array in mine]
    sums, panel = pl.pallas_call(
        functools.partial(gram_kernel, x_count),
        out_shape=[VMEM((count, 2 * count), f32), VMEM((2 * count, width), jnp.bfloat16)],
        in_specs=[in_vmem] * (2 * x_count + 1),
        out_specs=[in_vmem] * 2,
        name="gram",
    )(*map(near, mine), *map(near, other), near(trailing))
    steps = (1, 3, 4, 8, 28)
    for step in steps[:-1]:
        sums = sums + to_row(sums, step)
    far = to_row(sums, steps[-1])
    anywhere = pl.BlockSpec(memory_space=pl.ANY)
    large = (count, width)
    return pl.pallas_call(
        functools.partial(finish_kernel, root),
        out_shape=[jax.ShapeDtypeStruct((count, count), f32)] * 2
        + [jax.ShapeDtypeStruct(large, f32)] * 2,
        in_specs=[in_vmem] * 3 + [anywhere],
        out_specs=[in_vmem] * 2 + [anywhere] * 2,
        scratch_shapes=[VMEM(large, f32)] * 3
        + [pltpu.SemaphoreType.DMA(()), pltpu.SemaphoreType.DMA((4, 2))],
        name="finish",
    )(near(sums), near(far), near(panel), trailing)


def solution(mesh):
    placed = (P("col", "row"), P("col", "row"), P())
    return jax.shard_map(
        on_device,
        mesh=mesh,
        in_specs=placed,
        out_specs=(P(), P(None, "col"), P(None, "row"), P("col", "row")),
        check_vma=False,
    )
```

```python
import functools

import jax
import jax.numpy as jnp
import numpy as np
from jax import lax
from jax.experimental import pallas as pl
from jax.experimental.pallas import tpu as pltpu
from jax.sharding import PartitionSpec as P

VMEM = pltpu.VMEM
SMEM = pltpu.SMEM
CORES = 2


def split_bf16(value):
    high = value.astype(jnp.bfloat16)
    low = (value - high.astype(jnp.float32)).astype(jnp.bfloat16)
    return high, low


def select_kernel(x_count, pivots_ref, cand_ref, *rest):
    outs, (rows, sems) = rest[:x_count], rest[x_count:]
    cand_count, width = cand_ref.shape
    count = pivots_ref.shape[0]
    me = lax.axis_index("col")
    rows[...] = jnp.zeros_like(rows)

    def row_copy(pivot, slot):
        return pltpu.make_async_copy(
            cand_ref.at[pl.ds(pivot - me * cand_count, 1), :], rows.at[pl.ds(slot, 1), :], sems.at[slot]
        )

    def fetch(i, slot):
        pivot = pivots_ref[i]
        mine = pivot // cand_count == me

        @pl.when(mine)
        def _():
            row_copy(pivot, slot).start()

        return slot + mine.astype(jnp.int32)

    total = lax.fori_loop(0, count, fetch, jnp.int32(0), unroll=8)

    def drain(slot, carry):
        row_copy(me * cand_count, slot).wait()
        return carry

    lax.fori_loop(0, total, drain, 0)
    part = width // x_count
    for k in range(x_count):
        begin = pl.multiple_of(((me // CORES) ^ k) * part, part)
        outs[k][...] = rows[:, pl.ds(begin, part)]


def merge_kernel(x_count, keys_ref, *rest):
    sources, (keep_ref, send_ref) = rest[:x_count], rest[x_count:]
    count, half = keep_ref.shape
    held = x_count * sources[0].shape[0]
    my_core = lax.axis_index("col") % CORES
    lanes = lax.broadcasted_iota(jnp.int32, (count, held), 1)
    pick = (keys_ref[...] == lanes).astype(jnp.float32).astype(jnp.bfloat16)
    pick = jnp.concatenate([pick, pick], axis=1)
    for out_ref, core in ((send_ref, 1 - my_core), (keep_ref, my_core)):
        begin = pl.multiple_of(core * half, half)
        value = jnp.concatenate([ref[:, pl.ds(begin, half)] for ref in sources], axis=0)
        parts = jnp.concatenate(split_bf16(value), axis=0)
        out_ref[...] = jnp.dot(pick, parts, preferred_element_type=jnp.float32)


def gram_kernel(x_count, *rest):
    mine, other = rest[:x_count], rest[x_count : 2 * x_count]
    trail_ref, sums_ref, panel_ref = rest[2 * x_count :]
    count, piece = mine[0].shape
    width = trail_ref.shape[1]
    me = lax.axis_index("col")
    my_x, my_core = me // CORES, me % CORES
    for k in range(x_count):
        near_core = my_core if k == 0 else 1 - my_core
        for core, ref in ((near_core, mine[k]), (1 - near_core, other[k])):
            begin = pl.multiple_of(((my_x ^ k) * CORES + core) * piece, piece)
            high, low = split_bf16(ref[...])
            panel_ref[0:count, pl.ds(begin, piece)] = high
            panel_ref[count : 2 * count, pl.ds(begin, piece)] = low
    total = jnp.zeros((2 * count, 4 * count), jnp.float32)
    for begin in range(0, width, piece):
        block = slice(begin, begin + piece)
        trail_high, trail_low = split_bf16(trail_ref[:, block])
        panel_parts = panel_ref[:, block]
        right = jnp.concatenate(
            [panel_parts[:count], trail_high, panel_parts[count:], trail_low], axis=0
        )
        total += lax.dot_general(
            panel_parts, right, (((1,), (1,)), ((), ())), preferred_element_type=jnp.float32
        )
    lead = total[:count] + total[count:]
    sums_ref[...] = lead[:, : 2 * count] + lead[:, 2 * count :]


def outer_sum(left, right):
    def parts(value):
        first = value.astype(jnp.bfloat16).astype(jnp.float32)
        rest = value - first
        second = rest.astype(jnp.bfloat16).astype(jnp.float32)
        return first, second, rest - second

    l1, l2, l3 = parts(left)
    r1, r2, r3 = parts(right)
    return lax.dot_general(
        jnp.concatenate([l1, l1, l2, l2, l1, l3], axis=0).astype(jnp.bfloat16),
        jnp.concatenate([r1, r2, r1, r2, r3, r1], axis=0).astype(jnp.bfloat16),
        (((0,), (0,)), ((), ())),
        preferred_element_type=jnp.float32,
    )


def eliminate(work):
    size = 8
    count, width = work.shape
    shape = (size, width)
    blocks = [work[begin : begin + size] for begin in range(0, count, size)]
    rows = lax.broadcasted_iota(jnp.int32, shape, 0)
    lanes = lax.broadcasted_iota(jnp.int32, shape, 1)
    scales = []
    for b in range(len(blocks)):
        block = blocks[b]
        columns = [
            jnp.broadcast_to(block[:, size * b + k : size * b + k + 1], shape) for k in range(size)
        ]
        scale = jnp.zeros(shape, jnp.float32)
        for j in range(size):
            pivot = jnp.broadcast_to(columns[j][j : j + 1], shape)
            scale = jnp.where(rows == j, lax.rsqrt(pivot), scale)
            below = rows > j
            factor = jnp.where(below, columns[j] * (1.0 / pivot), 0.0)
            for k in range(j + 1, size):
                columns[k] -= factor * jnp.broadcast_to(columns[k][j : j + 1], shape)
            here = lanes == size * b + j
            row = jnp.where(here, 1.0, jnp.broadcast_to(block[j : j + 1], shape))
            block = jnp.where(here & below, 0.0, block) - factor * row
        block *= scale
        blocks[b] = block
        scales.append(scale)
        if b + 1 < len(blocks):
            place = lanes - size * b
            inside = (place >= 0) & (place < size)
            inverse = jnp.where(place < rows, block, jnp.where(place == rows, scale, 0.0))
            update = outer_sum(block[:, :count], jnp.where(inside, inverse, block))
            for c in range(b + 1, len(blocks)):
                blocks[c] = jnp.where(inside, 0.0, blocks[c]) - update[size * c : size * (c + 1)]
    return jnp.concatenate(blocks, axis=0), jnp.concatenate(scales, axis=0)


def finish_kernel(
    root, one_ref, two_ref, panel_ref, trail_ref, upper_ref, coef_ref, basis_ref, next_ref, trail, basis, left_over, in_sem, out_sems
):
    count = one_ref.shape[0]
    fetch = pltpu.make_async_copy(trail_ref, trail, in_sem)
    fetch.start()
    work, scale = eliminate(one_ref[...] + two_ref[...])
    square = (count, count)
    rows = lax.broadcasted_iota(jnp.int32, square, 0)
    lanes = lax.broadcasted_iota(jnp.int32, square, 1)
    factor, coef = work[:, :count], work[:, count:]
    upper_ref[...] = jnp.where(lanes >= rows, factor, 0.0) * jnp.float32(1.0 / root)
    coef_ref[...] = coef * jnp.float32(1.0 / root)
    inverse = jnp.where(lanes < rows, factor, jnp.where(lanes == rows, scale[:, :count], 0.0))
    weights = outer_sum(coef, inverse)
    high, low = split_bf16(jnp.concatenate([inverse * jnp.float32(root), weights], axis=0))
    left = jnp.concatenate([high, high, low, low], axis=1)
    fetch.wait()
    chunks = out_sems.shape[0]
    width = panel_ref.shape[1] // chunks
    copies = []
    for c in range(chunks):
        here = slice(c * width, (c + 1) * width)
        block = panel_ref[:, here]
        both = jnp.dot(
            left, jnp.concatenate([block, block], axis=0), preferred_element_type=jnp.float32
        )
        basis[:, here] = both[:count]
        left_over[:, here] = trail[:, here] - both[count:]
        for i, (source, target) in enumerate(((basis, basis_ref), (left_over, next_ref))):
            copy = pltpu.make_async_copy(source.at[:, here], target.at[:, here], out_sems.at[c, i])
            copy.start()
            copies.append(copy)
    for copy in copies:
        copy.wait()


def on_device(candidates, trailing, pivots):
    cand_count, width = candidates.shape
    count = pivots.shape[0]
    col_count, row_count = lax.axis_size("col"), lax.axis_size("row")
    x_count = col_count // CORES
    capacity = count // 2
    piece = width // col_count
    root = float(np.sqrt(np.float32(width * row_count)))
    my_col = lax.axis_index("col")
    owners = pivots // cand_count
    order = jnp.arange(count, dtype=jnp.int32)
    earlier = (owners[:, None] == owners[None, :]) & (order[None, :] < order[:, None])
    slots = jnp.sum(earlier.astype(jnp.int32), axis=1)
    away = (owners // CORES) ^ (my_col // CORES)
    held = (owners % CORES == my_col % CORES) == (away == 0)
    keys = jnp.where(held, away * capacity + slots, -1)[:, None]
    f32 = jnp.float32

    def to_x(array, k):
        return lax.ppermute(array, "col", [(i, i ^ (CORES * k + 1)) for i in range(col_count)])

    def to_core(array):
        return lax.ppermute(array, "col", [(i, i ^ 1) for i in range(col_count)])

    def to_row(array, k):
        return lax.ppermute(array, "row", [(i, i ^ k) for i in range(row_count)])

    def near(array):
        return pltpu.with_memory_space_constraint(array, VMEM)

    in_vmem, in_smem = pl.BlockSpec(memory_space=VMEM), pl.BlockSpec(memory_space=SMEM)
    quarters = pl.pallas_call(
        functools.partial(select_kernel, x_count),
        out_shape=[VMEM((capacity, width // x_count), f32)] * x_count,
        in_specs=[in_smem, pl.BlockSpec(memory_space=pl.ANY)],
        out_specs=[in_vmem] * x_count,
        scratch_shapes=[VMEM((capacity, width), f32), pltpu.SemaphoreType.DMA((capacity,))],
        name="select",
    )(pivots, candidates)
    arrived = [quarters[0]] + [to_x(quarters[k], k) for k in range(1, x_count)]
    keep, send = pl.pallas_call(
        functools.partial(merge_kernel, x_count),
        out_shape=[VMEM((count, piece), f32)] * 2,
        in_specs=[in_vmem] * (1 + x_count),
        out_specs=[in_vmem] * 2,
        name="merge",
    )(near(keys), *map(near, arrived))
    own_piece = keep + to_core(send)
    mine = [own_piece] + [to_x(own_piece, k) for k in range(1, x_count)]
    other = [to_core(array) for array in mine]
    sums, panel = pl.pallas_call(
        functools.partial(gram_kernel, x_count),
        out_shape=[VMEM((count, 2 * count), f32), VMEM((2 * count, width), jnp.bfloat16)],
        in_specs=[in_vmem] * (2 * x_count + 1),
        out_specs=[in_vmem] * 2,
        name="gram",
    )(*map(near, mine), *map(near, other), near(trailing))
    for step in (1, 4):
        sums = (sums + to_row(sums, step)) + (to_row(sums, 2 * step) + to_row(sums, 3 * step))
    far = to_row(sums, 28)
    anywhere = pl.BlockSpec(memory_space=pl.ANY)
    large = (count, width)
    return pl.pallas_call(
        functools.partial(finish_kernel, root),
        out_shape=[jax.ShapeDtypeStruct((count, count), f32)] * 2
        + [jax.ShapeDtypeStruct(large, f32)] * 2,
        in_specs=[in_vmem] * 3 + [anywhere],
        out_specs=[in_vmem] * 2 + [anywhere] * 2,
        scratch_shapes=[VMEM(large, f32)] * 3
        + [pltpu.SemaphoreType.DMA(()), pltpu.SemaphoreType.DMA((4, 2))],
        name="finish",
    )(near(sums), near(far), near(panel), trailing)


def solution(mesh):
    placed = (P("col", "row"), P("col", "row"), P())
    return jax.shard_map(
        on_device,
        mesh=mesh,
        in_specs=placed,
        out_specs=(P(), P(None, "col"), P(None, "row"), P("col", "row")),
        check_vma=False,
    )
```

```python
import functools

import jax
import jax.numpy as jnp
import numpy as np
from jax import lax
from jax.experimental import pallas as pl
from jax.experimental.pallas import tpu as pltpu
from jax.sharding import PartitionSpec as P

VMEM = pltpu.VMEM
SMEM = pltpu.SMEM
CORES = 2


def split_bf16(value):
    high = value.astype(jnp.bfloat16)
    low = (value - high.astype(jnp.float32)).astype(jnp.bfloat16)
    return high, low


def select_kernel(x_count, pivots_ref, cand_ref, *rest):
    outs, (rows, sems) = rest[:x_count], rest[x_count:]
    cand_count, width = cand_ref.shape
    count = pivots_ref.shape[0]
    me = lax.axis_index("col")
    rows[...] = jnp.zeros_like(rows)

    def row_copy(pivot, slot):
        return pltpu.make_async_copy(
            cand_ref.at[pl.ds(pivot - me * cand_count, 1), :], rows.at[pl.ds(slot, 1), :], sems.at[slot]
        )

    def fetch(i, slot):
        pivot = pivots_ref[i]
        mine = pivot // cand_count == me

        @pl.when(mine)
        def _():
            row_copy(pivot, slot).start()

        return slot + mine.astype(jnp.int32)

    total = lax.fori_loop(0, count, fetch, jnp.int32(0), unroll=8)

    def drain(slot, carry):
        row_copy(me * cand_count, slot).wait()
        return carry

    lax.fori_loop(0, total, drain, 0)
    part = width // x_count
    for k in range(x_count):
        begin = pl.multiple_of(((me // CORES) ^ k) * part, part)
        outs[k][...] = rows[:, pl.ds(begin, part)]


def merge_kernel(x_count, keys_ref, *rest):
    sources, (keep_ref, send_ref) = rest[:x_count], rest[x_count:]
    count, half = keep_ref.shape
    held = x_count * sources[0].shape[0]
    my_core = lax.axis_index("col") % CORES
    lanes = lax.broadcasted_iota(jnp.int32, (count, held), 1)
    pick = (keys_ref[...] == lanes).astype(jnp.float32).astype(jnp.bfloat16)
    pick = jnp.concatenate([pick, pick], axis=1)
    for out_ref, core in ((send_ref, 1 - my_core), (keep_ref, my_core)):
        begin = pl.multiple_of(core * half, half)
        value = jnp.concatenate([ref[:, pl.ds(begin, half)] for ref in sources], axis=0)
        parts = jnp.concatenate(split_bf16(value), axis=0)
        out_ref[...] = jnp.dot(pick, parts, preferred_element_type=jnp.float32)


def gram_kernel(x_count, *rest):
    mine, other = rest[:x_count], rest[x_count : 2 * x_count]
    trail_ref, sums_ref, panel_ref = rest[2 * x_count :]
    count, piece = mine[0].shape
    width = trail_ref.shape[1]
    me = lax.axis_index("col")
    my_x, my_core = me // CORES, me % CORES
    for k in range(x_count):
        near_core = my_core if k == 0 else 1 - my_core
        for core, ref in ((near_core, mine[k]), (1 - near_core, other[k])):
            begin = pl.multiple_of(((my_x ^ k) * CORES + core) * piece, piece)
            high, low = split_bf16(ref[...])
            panel_ref[0:count, pl.ds(begin, piece)] = high
            panel_ref[count : 2 * count, pl.ds(begin, piece)] = low
    total = jnp.zeros((2 * count, 4 * count), jnp.float32)
    for begin in range(0, width, piece):
        block = slice(begin, begin + piece)
        trail_high, trail_low = split_bf16(trail_ref[:, block])
        panel_parts = panel_ref[:, block]
        right = jnp.concatenate(
            [panel_parts[:count], trail_high, panel_parts[count:], trail_low], axis=0
        )
        total += lax.dot_general(
            panel_parts, right, (((1,), (1,)), ((), ())), preferred_element_type=jnp.float32
        )
    lead = total[:count] + total[count:]
    sums_ref[...] = lead[:, : 2 * count] + lead[:, 2 * count :]


def outer_sum(left, right):
    def parts(value):
        first = value.astype(jnp.bfloat16).astype(jnp.float32)
        rest = value - first
        second = rest.astype(jnp.bfloat16).astype(jnp.float32)
        return first, second, rest - second

    l1, l2, l3 = parts(left)
    r1, r2, r3 = parts(right)
    return lax.dot_general(
        jnp.concatenate([l1, l1, l2, l2, l1, l3], axis=0).astype(jnp.bfloat16),
        jnp.concatenate([r1, r2, r1, r2, r3, r1], axis=0).astype(jnp.bfloat16),
        (((0,), (0,)), ((), ())),
        preferred_element_type=jnp.float32,
    )


def eliminate(work):
    size = 8
    count, width = work.shape
    shape = (size, width)
    blocks = [work[begin : begin + size] for begin in range(0, count, size)]
    rows = lax.broadcasted_iota(jnp.int32, shape, 0)
    lanes = lax.broadcasted_iota(jnp.int32, shape, 1)
    scales = []
    for b in range(len(blocks)):
        block = blocks[b]
        columns = [
            jnp.broadcast_to(block[:, size * b + k : size * b + k + 1], shape) for k in range(size)
        ]
        scale = jnp.zeros(shape, jnp.float32)
        for j in range(size):
            pivot = jnp.broadcast_to(columns[j][j : j + 1], shape)
            scale = jnp.where(rows == j, lax.rsqrt(pivot), scale)
            below = rows > j
            factor = jnp.where(below, columns[j] * (1.0 / pivot), 0.0)
            for k in range(j + 1, size):
                columns[k] -= factor * jnp.broadcast_to(columns[k][j : j + 1], shape)
            here = lanes == size * b + j
            row = jnp.where(here, 1.0, jnp.broadcast_to(block[j : j + 1], shape))
            block = jnp.where(here & below, 0.0, block) - factor * row
        block *= scale
        blocks[b] = block
        scales.append(scale)
        if b + 1 < len(blocks):
            place = lanes - size * b
            inside = (place >= 0) & (place < size)
            inverse = jnp.where(place < rows, block, jnp.where(place == rows, scale, 0.0))
            update = outer_sum(block[:, :count], jnp.where(inside, inverse, block))
            for c in range(b + 1, len(blocks)):
                blocks[c] = jnp.where(inside, 0.0, blocks[c]) - update[size * c : size * (c + 1)]
    return jnp.concatenate(blocks, axis=0), jnp.concatenate(scales, axis=0)


def finish_kernel(
    root, one_ref, two_ref, panel_ref, trail_ref, upper_ref, coef_ref, basis_ref, next_ref, trail, basis, left_over, in_sem, out_sems
):
    count = one_ref.shape[0]
    fetch = pltpu.make_async_copy(trail_ref, trail, in_sem)
    fetch.start()
    work, scale = eliminate(one_ref[...] + two_ref[...])
    square = (count, count)
    rows = lax.broadcasted_iota(jnp.int32, square, 0)
    lanes = lax.broadcasted_iota(jnp.int32, square, 1)
    factor, coef = work[:, :count], work[:, count:]
    upper_ref[...] = jnp.where(lanes >= rows, factor, 0.0) * jnp.float32(1.0 / root)
    coef_ref[...] = coef * jnp.float32(1.0 / root)
    inverse = jnp.where(lanes < rows, factor, jnp.where(lanes == rows, scale[:, :count], 0.0))
    weights = outer_sum(coef, inverse)
    high, low = split_bf16(jnp.concatenate([inverse * jnp.float32(root), weights], axis=0))
    left = jnp.concatenate([high, high, low, low], axis=1)
    fetch.wait()
    chunks = out_sems.shape[0]
    width = panel_ref.shape[1] // chunks
    copies = []
    for c in range(chunks):
        here = slice(c * width, (c + 1) * width)
        block = panel_ref[:, here]
        both = jnp.dot(
            left, jnp.concatenate([block, block], axis=0), preferred_element_type=jnp.float32
        )
        basis[:, here] = both[:count]
        left_over[:, here] = trail[:, here] - both[count:]
        for i, (source, target) in enumerate(((basis, basis_ref), (left_over, next_ref))):
            copy = pltpu.make_async_copy(source.at[:, here], target.at[:, here], out_sems.at[c, i])
            copy.start()
            copies.append(copy)
    for copy in copies:
        copy.wait()


def on_device(candidates, trailing, pivots):
    cand_count, width = candidates.shape
    count = pivots.shape[0]
    col_count, row_count = lax.axis_size("col"), lax.axis_size("row")
    x_count = col_count // CORES
    capacity = count // 2
    piece = width // col_count
    root = float(np.sqrt(np.float32(width * row_count)))
    my_col = lax.axis_index("col")
    owners = pivots // cand_count
    order = jnp.arange(count, dtype=jnp.int32)
    earlier = (owners[:, None] == owners[None, :]) & (order[None, :] < order[:, None])
    slots = jnp.sum(earlier.astype(jnp.int32), axis=1)
    away = (owners // CORES) ^ (my_col // CORES)
    keys = jnp.where(owners % CORES == my_col % CORES, away * capacity + slots, -1)[:, None]
    f32 = jnp.float32

    def to_x(array, k, cross):
        return lax.ppermute(array, "col", [(i, i ^ (CORES * k + cross)) for i in range(col_count)])

    def to_core(array):
        return lax.ppermute(array, "col", [(i, i ^ 1) for i in range(col_count)])

    def to_row(array, k):
        return lax.ppermute(array, "row", [(i, i ^ k) for i in range(row_count)])

    def near(array):
        return pltpu.with_memory_space_constraint(array, VMEM)

    in_vmem, in_smem = pl.BlockSpec(memory_space=VMEM), pl.BlockSpec(memory_space=SMEM)
    quarters = pl.pallas_call(
        functools.partial(select_kernel, x_count),
        out_shape=[VMEM((capacity, width // x_count), f32)] * x_count,
        in_specs=[in_smem, pl.BlockSpec(memory_space=pl.ANY)],
        out_specs=[in_vmem] * x_count,
        scratch_shapes=[VMEM((capacity, width), f32), pltpu.SemaphoreType.DMA((capacity,))],
        name="select",
    )(pivots, candidates)
    arrived = [quarters[0]] + [to_x(quarters[k], k, 0) for k in range(1, x_count)]
    keep, send = pl.pallas_call(
        functools.partial(merge_kernel, x_count),
        out_shape=[VMEM((count, piece), f32)] * 2,
        in_specs=[in_vmem] * (1 + x_count),
        out_specs=[in_vmem] * 2,
        name="merge",
    )(near(keys), *map(near, arrived))
    own_piece = keep + to_core(send)
    mine = [own_piece] + [to_x(own_piece, k, 1) for k in range(1, x_count)]
    other = [to_core(array) for array in mine]
    sums, panel = pl.pallas_call(
        functools.partial(gram_kernel, x_count),
        out_shape=[VMEM((count, 2 * count), f32), VMEM((2 * count, width), jnp.bfloat16)],
        in_specs=[in_vmem] * (2 * x_count + 1),
        out_specs=[in_vmem] * 2,
        name="gram",
    )(*map(near, mine), *map(near, other), near(trailing))
    for one, two in ((1, 3), (4, 28)):
        sums = (sums + to_row(sums, one)) + (to_row(sums, two) + to_row(sums, one ^ two))
    far = to_row(sums, 8)
    anywhere = pl.BlockSpec(memory_space=pl.ANY)
    large = (count, width)
    return pl.pallas_call(
        functools.partial(finish_kernel, root),
        out_shape=[jax.ShapeDtypeStruct((count, count), f32)] * 2
        + [jax.ShapeDtypeStruct(large, f32)] * 2,
        in_specs=[in_vmem] * 3 + [anywhere],
        out_specs=[in_vmem] * 2 + [anywhere] * 2,
        scratch_shapes=[VMEM(large, f32)] * 3
        + [pltpu.SemaphoreType.DMA(()), pltpu.SemaphoreType.DMA((4, 2))],
        name="finish",
    )(near(sums), near(far), near(panel), trailing)


def solution(mesh):
    placed = (P("col", "row"), P("col", "row"), P())
    return jax.shard_map(
        on_device,
        mesh=mesh,
        in_specs=placed,
        out_specs=(P(), P(None, "col"), P(None, "row"), P("col", "row")),
        check_vma=False,
    )
```

```python
import functools

import jax
import jax.numpy as jnp
import numpy as np
from jax import lax
from jax.experimental import pallas as pl
from jax.experimental.pallas import tpu as pltpu
from jax.sharding import PartitionSpec as P

VMEM = pltpu.VMEM
SMEM = pltpu.SMEM
CORES = 2


def split_bf16(value):
    high = value.astype(jnp.bfloat16)
    low = (value - high.astype(jnp.float32)).astype(jnp.bfloat16)
    return high, low


def select_kernel(x_count, pivots_ref, cand_ref, *rest):
    outs, (rows, sems) = rest[:x_count], rest[x_count:]
    cand_count, width = cand_ref.shape
    count = pivots_ref.shape[0]
    me = lax.axis_index("col")
    first = me * cand_count
    rows[...] = jnp.zeros_like(rows)

    def row_copy(pivot, slot):
        return pltpu.make_async_copy(
            cand_ref.at[pl.ds(pivot - first, 1), :], rows.at[pl.ds(slot, 1), :], sems.at[slot]
        )

    def fetch(i, slot):
        pivot = pivots_ref[i]
        mine = (pivot >= first) & (pivot < first + cand_count)

        @pl.when(mine)
        def _():
            row_copy(pivot, slot).start()

        return slot + mine.astype(jnp.int32)

    total = lax.fori_loop(0, count, fetch, jnp.int32(0), unroll=8)

    def drain(slot, carry):
        row_copy(first, slot).wait()
        return carry

    lax.fori_loop(0, total, drain, 0)
    part = width // x_count
    for k in range(x_count):
        begin = pl.multiple_of(((me // CORES) ^ k) * part, part)
        outs[k][...] = rows[:, pl.ds(begin, part)]


def merge_kernel(x_count, keys_ref, *rest):
    sources, (keep_ref, send_ref) = rest[:x_count], rest[x_count:]
    count, half = keep_ref.shape
    held = x_count * sources[0].shape[0]
    my_core = lax.axis_index("col") % CORES
    lanes = lax.broadcasted_iota(jnp.int32, (count, held), 1)
    pick = (keys_ref[...] == lanes).astype(jnp.float32).astype(jnp.bfloat16)
    pick = jnp.concatenate([pick, pick], axis=1)
    for out_ref, core in ((send_ref, 1 - my_core), (keep_ref, my_core)):
        begin = pl.multiple_of(core * half, half)
        value = jnp.concatenate([ref[:, pl.ds(begin, half)] for ref in sources], axis=0)
        parts = jnp.concatenate(split_bf16(value), axis=0)
        out_ref[...] = jnp.dot(pick, parts, preferred_element_type=jnp.float32)


def gram_kernel(x_count, *rest):
    mine, other = rest[:x_count], rest[x_count : 2 * x_count]
    trail_ref, sums_ref, panel_ref = rest[2 * x_count :]
    count, piece = mine[0].shape
    width = trail_ref.shape[1]
    me = lax.axis_index("col")
    my_x, my_core = me // CORES, me % CORES
    for k in range(x_count):
        near_core = my_core
        for core, ref in ((near_core, mine[k]), (1 - near_core, other[k])):
            begin = pl.multiple_of(((my_x ^ k) * CORES + core) * piece, piece)
            high, low = split_bf16(ref[...])
            panel_ref[0:count, pl.ds(begin, piece)] = high
            panel_ref[count : 2 * count, pl.ds(begin, piece)] = low
    total = jnp.zeros((2 * count, 4 * count), jnp.float32)
    for begin in range(0, width, piece):
        block = slice(begin, begin + piece)
        trail_high, trail_low = split_bf16(trail_ref[:, block])
        panel_parts = panel_ref[:, block]
        right = jnp.concatenate(
            [panel_parts[:count], trail_high, panel_parts[count:], trail_low], axis=0
        )
        total += lax.dot_general(
            panel_parts, right, (((1,), (1,)), ((), ())), preferred_element_type=jnp.float32
        )
    lead = total[:count] + total[count:]
    sums_ref[...] = lead[:, : 2 * count] + lead[:, 2 * count :]


def outer_sum(left, right):
    def parts(value):
        first = value.astype(jnp.bfloat16).astype(jnp.float32)
        rest = value - first
        second = rest.astype(jnp.bfloat16).astype(jnp.float32)
        return first, second, rest - second

    l1, l2, l3 = parts(left)
    r1, r2, r3 = parts(right)
    return lax.dot_general(
        jnp.concatenate([l1, l1, l2, l2, l1, l3], axis=0).astype(jnp.bfloat16),
        jnp.concatenate([r1, r2, r1, r2, r3, r1], axis=0).astype(jnp.bfloat16),
        (((0,), (0,)), ((), ())),
        preferred_element_type=jnp.float32,
    )


def eliminate(work):
    size = 8
    count, width = work.shape
    shape = (size, width)
    blocks = [work[begin : begin + size] for begin in range(0, count, size)]
    rows = lax.broadcasted_iota(jnp.int32, shape, 0)
    lanes = lax.broadcasted_iota(jnp.int32, shape, 1)
    scales = []
    for b in range(len(blocks)):
        block = blocks[b]
        columns = [
            jnp.broadcast_to(block[:, size * b + k : size * b + k + 1], shape) for k in range(size)
        ]
        scale = jnp.zeros(shape, jnp.float32)
        for j in range(size):
            pivot = jnp.broadcast_to(columns[j][j : j + 1], shape)
            scale = jnp.where(rows == j, lax.rsqrt(pivot), scale)
            below = rows > j
            factor = jnp.where(below, columns[j] * (1.0 / pivot), 0.0)
            for k in range(j + 1, size):
                columns[k] -= factor * jnp.broadcast_to(columns[k][j : j + 1], shape)
            here = lanes == size * b + j
            row = jnp.where(here, 1.0, jnp.broadcast_to(block[j : j + 1], shape))
            block = jnp.where(here & below, 0.0, block) - factor * row
        block *= scale
        blocks[b] = block
        scales.append(scale)
        if b + 1 < len(blocks):
            place = lanes - size * b
            inside = (place >= 0) & (place < size)
            inverse = jnp.where(place < rows, block, jnp.where(place == rows, scale, 0.0))
            update = outer_sum(block[:, :count], jnp.where(inside, inverse, block))
            for c in range(b + 1, len(blocks)):
                blocks[c] = jnp.where(inside, 0.0, blocks[c]) - update[size * c : size * (c + 1)]
    return jnp.concatenate(blocks, axis=0), jnp.concatenate(scales, axis=0)


def finish_kernel(
    root, one_ref, two_ref, panel_ref, trail_ref, upper_ref, coef_ref, basis_ref, next_ref, trail, basis, left_over, in_sem, out_sems
):
    count = one_ref.shape[0]
    fetch = pltpu.make_async_copy(trail_ref, trail, in_sem)
    fetch.start()
    work, scale = eliminate(one_ref[...] + two_ref[...])
    square = (count, count)
    rows = lax.broadcasted_iota(jnp.int32, square, 0)
    lanes = lax.broadcasted_iota(jnp.int32, square, 1)
    factor, coef = work[:, :count], work[:, count:]
    upper_ref[...] = jnp.where(lanes >= rows, factor, 0.0) * jnp.float32(1.0 / root)
    coef_ref[...] = coef * jnp.float32(1.0 / root)
    inverse = jnp.where(lanes < rows, factor, jnp.where(lanes == rows, scale[:, :count], 0.0))
    weights = outer_sum(coef, inverse)
    high, low = split_bf16(jnp.concatenate([inverse * jnp.float32(root), weights], axis=0))
    left = jnp.concatenate([high, high, low, low], axis=1)
    fetch.wait()
    chunks = out_sems.shape[0]
    width = panel_ref.shape[1] // chunks
    copies = []
    for c in range(chunks):
        here = slice(c * width, (c + 1) * width)
        block = panel_ref[:, here]
        both = jnp.dot(
            left, jnp.concatenate([block, block], axis=0), preferred_element_type=jnp.float32
        )
        basis[:, here] = both[:count]
        left_over[:, here] = trail[:, here] - both[count:]
        for i, (source, target) in enumerate(((basis, basis_ref), (left_over, next_ref))):
            copy = pltpu.make_async_copy(source.at[:, here], target.at[:, here], out_sems.at[c, i])
            copy.start()
            copies.append(copy)
    for copy in copies:
        copy.wait()


def on_device(candidates, trailing, pivots):
    cand_count, width = candidates.shape
    count = pivots.shape[0]
    col_count, row_count = lax.axis_size("col"), lax.axis_size("row")
    x_count = col_count // CORES
    capacity = count // 2
    piece = width // col_count
    root = float(np.sqrt(np.float32(width * row_count)))
    my_col = lax.axis_index("col")
    owners = pivots // cand_count
    order = jnp.arange(count, dtype=jnp.int32)
    earlier = (owners[:, None] == owners[None, :]) & (order[None, :] < order[:, None])
    slots = jnp.sum(earlier.astype(jnp.int32), axis=1)
    away = (owners // CORES) ^ (my_col // CORES)
    keys = jnp.where(owners % CORES == my_col % CORES, away * capacity + slots, -1)[:, None]
    f32 = jnp.float32

    def to_x(array, k, cross):
        return lax.ppermute(array, "col", [(i, i ^ (CORES * k + cross)) for i in range(col_count)])

    def to_core(array):
        return lax.ppermute(array, "col", [(i, i ^ 1) for i in range(col_count)])

    def to_row(array, k):
        return lax.ppermute(array, "row", [(i, i ^ k) for i in range(row_count)])

    def near(array):
        return pltpu.with_memory_space_constraint(array, VMEM)

    in_vmem, in_smem = pl.BlockSpec(memory_space=VMEM), pl.BlockSpec(memory_space=SMEM)
    quarters = pl.pallas_call(
        functools.partial(select_kernel, x_count),
        out_shape=[VMEM((capacity, width // x_count), f32)] * x_count,
        in_specs=[in_smem, pl.BlockSpec(memory_space=pl.ANY)],
        out_specs=[in_vmem] * x_count,
        scratch_shapes=[VMEM((capacity, width), f32), pltpu.SemaphoreType.DMA((capacity,))],
        name="select",
    )(pivots, candidates)
    arrived = [quarters[0]] + [to_x(quarters[k], k, 0) for k in range(1, x_count)]
    keep, send = pl.pallas_call(
        functools.partial(merge_kernel, x_count),
        out_shape=[VMEM((count, piece), f32)] * 2,
        in_specs=[in_vmem] * (1 + x_count),
        out_specs=[in_vmem] * 2,
        name="merge",
    )(near(keys), *map(near, arrived))
    own_piece = keep + to_core(send)
    mine = [own_piece] + [to_x(own_piece, k, 0) for k in range(1, x_count)]
    other = [to_core(array) for array in mine]
    sums, panel = pl.pallas_call(
        functools.partial(gram_kernel, x_count),
        out_shape=[VMEM((count, 2 * count), f32), VMEM((2 * count, width), jnp.bfloat16)],
        in_specs=[in_vmem] * (2 * x_count + 1),
        out_specs=[in_vmem] * 2,
        name="gram",
    )(*map(near, mine), *map(near, other), near(trailing))
    for partners in ((1, 2, 3), (4, 8, 12)):
        terms = [sums] + [to_row(sums, k) for k in partners]
        while len(terms) > 1:
            terms = [one + two for one, two in zip(terms[::2], terms[1::2])]
        sums = terms[0]
    far = to_row(sums, 28)
    anywhere = pl.BlockSpec(memory_space=pl.ANY)
    large = (count, width)
    return pl.pallas_call(
        functools.partial(finish_kernel, root),
        out_shape=[jax.ShapeDtypeStruct((count, count), f32)] * 2
        + [jax.ShapeDtypeStruct(large, f32)] * 2,
        in_specs=[in_vmem] * 3 + [anywhere],
        out_specs=[in_vmem] * 2 + [anywhere] * 2,
        scratch_shapes=[VMEM(large, f32)] * 3
        + [pltpu.SemaphoreType.DMA(()), pltpu.SemaphoreType.DMA((4, 2))],
        name="finish",
    )(near(sums), near(far), near(panel), trailing)


def solution(mesh):
    placed = (P("col", "row"), P("col", "row"), P())
    return jax.shard_map(
        on_device,
        mesh=mesh,
        in_specs=placed,
        out_specs=(P(), P(None, "col"), P(None, "row"), P("col", "row")),
        check_vma=False,
    )
```

```python
import functools

import jax
import jax.numpy as jnp
import numpy as np
from jax import lax
from jax.experimental import pallas as pl
from jax.experimental.pallas import tpu as pltpu
from jax.sharding import PartitionSpec as P

VMEM = pltpu.VMEM
SMEM = pltpu.SMEM
CORES = 2


def split_bf16(value):
    high = value.astype(jnp.bfloat16)
    low = (value - high.astype(jnp.float32)).astype(jnp.bfloat16)
    return high, low


def select_kernel(x_count, pivots_ref, cand_ref, *rest):
    outs, (rows, sems) = rest[:x_count], rest[x_count:]
    cand_count, width = cand_ref.shape
    count = pivots_ref.shape[0]
    me = lax.axis_index("col")
    first = me * cand_count
    rows[...] = jnp.zeros_like(rows)

    def row_copy(pivot, slot):
        return pltpu.make_async_copy(
            cand_ref.at[pl.ds(pivot - first, 1), :], rows.at[pl.ds(slot, 1), :], sems.at[slot]
        )

    def fetch(i, slot):
        pivot = pivots_ref[i]
        mine = (pivot >= first) & (pivot < first + cand_count)

        @pl.when(mine)
        def _():
            row_copy(pivot, slot).start()

        return slot + mine.astype(jnp.int32)

    total = lax.fori_loop(0, count, fetch, jnp.int32(0), unroll=8)

    def drain(slot, carry):
        row_copy(first, slot).wait()
        return carry

    lax.fori_loop(0, total, drain, 0)
    part = width // x_count
    for k in range(x_count):
        begin = pl.multiple_of(((me // CORES) ^ k) * part, part)
        outs[k][...] = rows[:, pl.ds(begin, part)]


def merge_kernel(x_count, keys_ref, *rest):
    sources, (keep_ref, send_ref) = rest[:x_count], rest[x_count:]
    count, half = keep_ref.shape
    held = x_count * sources[0].shape[0]
    my_core = lax.axis_index("col") % CORES
    lanes = lax.broadcasted_iota(jnp.int32, (count, held), 1)
    pick = (keys_ref[...] == lanes).astype(jnp.float32).astype(jnp.bfloat16)
    pick = jnp.concatenate([pick, pick], axis=1)
    for out_ref, core in ((send_ref, 1 - my_core), (keep_ref, my_core)):
        begin = pl.multiple_of(core * half, half)
        value = jnp.concatenate([ref[:, pl.ds(begin, half)] for ref in sources], axis=0)
        parts = jnp.concatenate(split_bf16(value), axis=0)
        out_ref[...] = jnp.dot(pick, parts, preferred_element_type=jnp.float32)


def gram_kernel(x_count, *rest):
    mine, other = rest[:x_count], rest[x_count : 2 * x_count]
    trail_ref, sums_ref, panel_ref = rest[2 * x_count :]
    count, piece = mine[0].shape
    width = trail_ref.shape[1]
    me = lax.axis_index("col")
    my_x, my_core = me // CORES, me % CORES
    for k in range(x_count):
        near_core = my_core
        for core, ref in ((near_core, mine[k]), (1 - near_core, other[k])):
            begin = pl.multiple_of(((my_x ^ k) * CORES + core) * piece, piece)
            high, low = split_bf16(ref[...])
            panel_ref[0:count, pl.ds(begin, piece)] = high
            panel_ref[count : 2 * count, pl.ds(begin, piece)] = low
    total = jnp.zeros((2 * count, 4 * count), jnp.float32)
    for begin in range(0, width, piece):
        block = slice(begin, begin + piece)
        trail_high, trail_low = split_bf16(trail_ref[:, block])
        panel_parts = panel_ref[:, block]
        right = jnp.concatenate(
            [panel_parts[:count], trail_high, panel_parts[count:], trail_low], axis=0
        )
        total += lax.dot_general(
            panel_parts, right, (((1,), (1,)), ((), ())), preferred_element_type=jnp.float32
        )
    lead = total[:count] + total[count:]
    sums_ref[...] = lead[:, : 2 * count] + lead[:, 2 * count :]


def outer_sum(left, right):
    def parts(value):
        first = value.astype(jnp.bfloat16).astype(jnp.float32)
        rest = value - first
        second = rest.astype(jnp.bfloat16).astype(jnp.float32)
        return first, second, rest - second

    l1, l2, l3 = parts(left)
    r1, r2, r3 = parts(right)
    return lax.dot_general(
        jnp.concatenate([l1, l1, l2, l2, l1, l3], axis=0).astype(jnp.bfloat16),
        jnp.concatenate([r1, r2, r1, r2, r3, r1], axis=0).astype(jnp.bfloat16),
        (((0,), (0,)), ((), ())),
        preferred_element_type=jnp.float32,
    )


def eliminate(work):
    size = 8
    count, width = work.shape
    shape = (size, width)
    blocks = [work[begin : begin + size] for begin in range(0, count, size)]
    rows = lax.broadcasted_iota(jnp.int32, shape, 0)
    lanes = lax.broadcasted_iota(jnp.int32, shape, 1)
    scales = []
    for b in range(len(blocks)):
        block = blocks[b]
        columns = [
            jnp.broadcast_to(block[:, size * b + k : size * b + k + 1], shape) for k in range(size)
        ]
        scale = jnp.zeros(shape, jnp.float32)
        for j in range(size):
            pivot = jnp.broadcast_to(columns[j][j : j + 1], shape)
            scale = jnp.where(rows == j, lax.rsqrt(pivot), scale)
            below = rows > j
            factor = jnp.where(below, columns[j] * (1.0 / pivot), 0.0)
            for k in range(j + 1, size):
                columns[k] -= factor * jnp.broadcast_to(columns[k][j : j + 1], shape)
            here = lanes == size * b + j
            row = jnp.where(here, 1.0, jnp.broadcast_to(block[j : j + 1], shape))
            block = jnp.where(here & below, 0.0, block) - factor * row
        block *= scale
        blocks[b] = block
        scales.append(scale)
        if b + 1 < len(blocks):
            place = lanes - size * b
            inside = (place >= 0) & (place < size)
            inverse = jnp.where(place < rows, block, jnp.where(place == rows, scale, 0.0))
            update = outer_sum(block[:, :count], jnp.where(inside, inverse, block))
            for c in range(b + 1, len(blocks)):
                blocks[c] = jnp.where(inside, 0.0, blocks[c]) - update[size * c : size * (c + 1)]
    return jnp.concatenate(blocks, axis=0), jnp.concatenate(scales, axis=0)


def finish_kernel(root, one_ref, two_ref, panel_ref, trail_ref, *rest):
    upper_ref, coef_ref, basis_ref, next_ref = rest[:4]
    upper, coef_out, trail, basis, left_over, in_sem, small_sems, out_sems = rest[4:]
    count = one_ref.shape[0]
    fetch = pltpu.make_async_copy(trail_ref, trail, in_sem)
    fetch.start()
    work, scale = eliminate(one_ref[...] + two_ref[...])
    square = (count, count)
    rows = lax.broadcasted_iota(jnp.int32, square, 0)
    lanes = lax.broadcasted_iota(jnp.int32, square, 1)
    factor, coef = work[:, :count], work[:, count:]
    upper[...] = jnp.where(lanes >= rows, factor, 0.0) * jnp.float32(1.0 / root)
    coef_out[...] = coef * jnp.float32(1.0 / root)
    copies = []
    for i, (source, target) in enumerate(((upper, upper_ref), (coef_out, coef_ref))):
        copy = pltpu.make_async_copy(source, target, small_sems.at[i])
        copy.start()
        copies.append(copy)
    inverse = jnp.where(lanes < rows, factor, jnp.where(lanes == rows, scale[:, :count], 0.0))
    weights = outer_sum(coef, inverse)
    high, low = split_bf16(jnp.concatenate([inverse * jnp.float32(root), weights], axis=0))
    left = jnp.concatenate([high, high, low, low], axis=1)
    fetch.wait()
    chunks = out_sems.shape[0]
    width = panel_ref.shape[1] // chunks
    for c in range(chunks):
        here = slice(c * width, (c + 1) * width)
        block = panel_ref[:, here]
        both = jnp.dot(
            left, jnp.concatenate([block, block], axis=0), preferred_element_type=jnp.float32
        )
        basis[:, here] = both[:count]
        left_over[:, here] = trail[:, here] - both[count:]
        for i, (source, target) in enumerate(((basis, basis_ref), (left_over, next_ref))):
            copy = pltpu.make_async_copy(source.at[:, here], target.at[:, here], out_sems.at[c, i])
            copy.start()
            copies.append(copy)
    for copy in copies:
        copy.wait()


def on_device(candidates, trailing, pivots):
    cand_count, width = candidates.shape
    count = pivots.shape[0]
    col_count, row_count = lax.axis_size("col"), lax.axis_size("row")
    x_count = col_count // CORES
    capacity = count // 2
    piece = width // col_count
    root = float(np.sqrt(np.float32(width * row_count)))
    my_col = lax.axis_index("col")
    owners = pivots // cand_count
    order = jnp.arange(count, dtype=jnp.int32)
    earlier = (owners[:, None] == owners[None, :]) & (order[None, :] < order[:, None])
    slots = jnp.sum(earlier.astype(jnp.int32), axis=1)
    away = (owners // CORES) ^ (my_col // CORES)
    keys = jnp.where(owners % CORES == my_col % CORES, away * capacity + slots, -1)[:, None]
    f32 = jnp.float32

    def to_x(array, k, cross):
        return lax.ppermute(array, "col", [(i, i ^ (CORES * k + cross)) for i in range(col_count)])

    def to_core(array):
        return lax.ppermute(array, "col", [(i, i ^ 1) for i in range(col_count)])

    def to_row(array, k):
        return lax.ppermute(array, "row", [(i, i ^ k) for i in range(row_count)])

    def near(array):
        return pltpu.with_memory_space_constraint(array, VMEM)

    in_vmem, in_smem = pl.BlockSpec(memory_space=VMEM), pl.BlockSpec(memory_space=SMEM)
    quarters = pl.pallas_call(
        functools.partial(select_kernel, x_count),
        out_shape=[VMEM((capacity, width // x_count), f32)] * x_count,
        in_specs=[in_smem, pl.BlockSpec(memory_space=pl.ANY)],
        out_specs=[in_vmem] * x_count,
        scratch_shapes=[VMEM((capacity, width), f32), pltpu.SemaphoreType.DMA((capacity,))],
        name="select",
    )(pivots, candidates)
    arrived = [quarters[0]] + [to_x(quarters[k], k, 0) for k in range(1, x_count)]
    keep, send = pl.pallas_call(
        functools.partial(merge_kernel, x_count),
        out_shape=[VMEM((count, piece), f32)] * 2,
        in_specs=[in_vmem] * (1 + x_count),
        out_specs=[in_vmem] * 2,
        name="merge",
    )(near(keys), *map(near, arrived))
    own_piece = keep + to_core(send)
    mine = [own_piece] + [to_x(own_piece, k, 0) for k in range(1, x_count)]
    other = [to_core(array) for array in mine]
    sums, panel = pl.pallas_call(
        functools.partial(gram_kernel, x_count),
        out_shape=[VMEM((count, 2 * count), f32), VMEM((2 * count, width), jnp.bfloat16)],
        in_specs=[in_vmem] * (2 * x_count + 1),
        out_specs=[in_vmem] * 2,
        name="gram",
    )(*map(near, mine), *map(near, other), near(trailing))
    for partners in ((1, 2, 3), (4, 8, 12)):
        terms = [sums] + [to_row(sums, k) for k in partners]
        while len(terms) > 1:
            terms = [one + two for one, two in zip(terms[::2], terms[1::2])]
        sums = terms[0]
    far = to_row(sums, 28)
    anywhere = pl.BlockSpec(memory_space=pl.ANY)
    large = (count, width)
    return pl.pallas_call(
        functools.partial(finish_kernel, root),
        out_shape=[jax.ShapeDtypeStruct((count, count), f32)] * 2
        + [jax.ShapeDtypeStruct(large, f32)] * 2,
        in_specs=[in_vmem] * 3 + [anywhere],
        out_specs=[anywhere] * 4,
        scratch_shapes=[VMEM((count, count), f32)] * 2
        + [VMEM(large, f32)] * 3
        + [pltpu.SemaphoreType.DMA(shape) for shape in ((), (2,), (4, 2))],
        name="finish",
    )(near(sums), near(far), near(panel), trailing)


def solution(mesh):
    placed = (P("col", "row"), P("col", "row"), P())
    return jax.shard_map(
        on_device,
        mesh=mesh,
        in_specs=placed,
        out_specs=(P(), P(None, "col"), P(None, "row"), P("col", "row")),
        check_vma=False,
    )
```

```python
import functools

import jax
import jax.numpy as jnp
import numpy as np
from jax import lax
from jax.experimental import pallas as pl
from jax.experimental.pallas import tpu as pltpu
from jax.sharding import PartitionSpec as P

VMEM = pltpu.VMEM
SMEM = pltpu.SMEM
CORES = 2


def split_bf16(value):
    high = value.astype(jnp.bfloat16)
    low = (value - high.astype(jnp.float32)).astype(jnp.bfloat16)
    return high, low


def select_kernel(x_count, pivots_ref, cand_ref, *rest):
    outs, (rows, sems) = rest[:x_count], rest[x_count:]
    cand_count, width = cand_ref.shape
    count = pivots_ref.shape[0]
    me = lax.axis_index("col")
    first = me * cand_count
    rows[...] = jnp.zeros_like(rows)

    def row_copy(pivot, slot):
        return pltpu.make_async_copy(
            cand_ref.at[pl.ds(pivot - first, 1), :], rows.at[pl.ds(slot, 1), :], sems.at[slot]
        )

    def fetch(i, slot):
        pivot = pivots_ref[i]
        mine = (pivot >= first) & (pivot < first + cand_count)

        @pl.when(mine)
        def _():
            row_copy(pivot, slot).start()

        return slot + mine.astype(jnp.int32)

    total = lax.fori_loop(0, count, fetch, jnp.int32(0), unroll=8)

    def drain(slot, carry):
        row_copy(first, slot).wait()
        return carry

    lax.fori_loop(0, total, drain, 0)
    part = width // x_count
    for k in range(x_count):
        begin = pl.multiple_of(((me // CORES) ^ k) * part, part)
        outs[k][...] = rows[:, pl.ds(begin, part)]


def merge_kernel(x_count, keys_ref, *rest):
    sources, (keep_ref, send_ref) = rest[:x_count], rest[x_count:]
    count, half = keep_ref.shape
    held = x_count * sources[0].shape[0]
    my_core = lax.axis_index("col") % CORES
    lanes = lax.broadcasted_iota(jnp.int32, (count, held), 1)
    pick = (keys_ref[...] == lanes).astype(jnp.float32).astype(jnp.bfloat16)
    pick = jnp.concatenate([pick, pick], axis=1)
    for out_ref, core in ((send_ref, 1 - my_core), (keep_ref, my_core)):
        begin = pl.multiple_of(core * half, half)
        value = jnp.concatenate([ref[:, pl.ds(begin, half)] for ref in sources], axis=0)
        parts = jnp.concatenate(split_bf16(value), axis=0)
        out_ref[...] = jnp.dot(pick, parts, preferred_element_type=jnp.float32)


def gram_kernel(x_count, *rest):
    mine, other = rest[:x_count], rest[x_count : 2 * x_count]
    trail_ref, sums_ref, panel_ref = rest[2 * x_count :]
    count, piece = mine[0].shape
    width = trail_ref.shape[1]
    me = lax.axis_index("col")
    my_x, my_core = me // CORES, me % CORES
    for k in range(x_count):
        near_core = my_core
        for core, ref in ((near_core, mine[k]), (1 - near_core, other[k])):
            begin = pl.multiple_of(((my_x ^ k) * CORES + core) * piece, piece)
            high, low = split_bf16(ref[...])
            panel_ref[0:count, pl.ds(begin, piece)] = high
            panel_ref[count : 2 * count, pl.ds(begin, piece)] = low
    total = jnp.zeros((2 * count, 4 * count), jnp.float32)
    for begin in range(0, width, piece):
        block = slice(begin, begin + piece)
        trail_high, trail_low = split_bf16(trail_ref[:, block])
        panel_parts = panel_ref[:, block]
        right = jnp.concatenate(
            [panel_parts[:count], trail_high, panel_parts[count:], trail_low], axis=0
        )
        total += lax.dot_general(
            panel_parts, right, (((1,), (1,)), ((), ())), preferred_element_type=jnp.float32
        )
    lead = total[:count] + total[count:]
    sums_ref[...] = lead[:, : 2 * count] + lead[:, 2 * count :]


def outer_sum(left, right):
    def parts(value):
        first = value.astype(jnp.bfloat16).astype(jnp.float32)
        rest = value - first
        second = rest.astype(jnp.bfloat16).astype(jnp.float32)
        return first, second, rest - second

    l1, l2, l3 = parts(left)
    r1, r2, r3 = parts(right)
    return lax.dot_general(
        jnp.concatenate([l1, l1, l2, l2, l1, l3], axis=0).astype(jnp.bfloat16),
        jnp.concatenate([r1, r2, r1, r2, r3, r1], axis=0).astype(jnp.bfloat16),
        (((0,), (0,)), ((), ())),
        preferred_element_type=jnp.float32,
    )


def eliminate(work):
    size = 32
    count, width = work.shape
    shape = (size, width)
    blocks = [work[begin : begin + size] for begin in range(0, count, size)]
    rows = lax.broadcasted_iota(jnp.int32, shape, 0)
    lanes = lax.broadcasted_iota(jnp.int32, shape, 1)
    scales = []
    for b in range(len(blocks)):
        block = blocks[b]
        columns = [
            jnp.broadcast_to(block[:, size * b + k : size * b + k + 1], shape) for k in range(size)
        ]
        scale = jnp.zeros(shape, jnp.float32)
        for j in range(size):
            pivot = jnp.broadcast_to(columns[j][j : j + 1], shape)
            scale = jnp.where(rows == j, lax.rsqrt(pivot), scale)
            below = rows > j
            factor = jnp.where(below, columns[j] * (1.0 / pivot), 0.0)
            for k in range(j + 1, size):
                columns[k] -= factor * jnp.broadcast_to(columns[k][j : j + 1], shape)
            here = lanes == size * b + j
            row = jnp.where(here, 1.0, jnp.broadcast_to(block[j : j + 1], shape))
            block = jnp.where(here & below, 0.0, block) - factor * row
        block *= scale
        blocks[b] = block
        scales.append(scale)
        if b + 1 < len(blocks):
            place = lanes - size * b
            inside = (place >= 0) & (place < size)
            inverse = jnp.where(place < rows, block, jnp.where(place == rows, scale, 0.0))
            update = outer_sum(block[:, :count], jnp.where(inside, inverse, block))
            for c in range(b + 1, len(blocks)):
                blocks[c] = jnp.where(inside, 0.0, blocks[c]) - update[size * c : size * (c + 1)]
    return jnp.concatenate(blocks, axis=0), jnp.concatenate(scales, axis=0)


def finish_kernel(root, one_ref, two_ref, panel_ref, trail_ref, *rest):
    upper_ref, coef_ref, basis_ref, next_ref = rest[:4]
    upper, coef_out, trail, basis, left_over, in_sem, small_sems, out_sems = rest[4:]
    count = one_ref.shape[0]
    fetch = pltpu.make_async_copy(trail_ref, trail, in_sem)
    fetch.start()
    work, scale = eliminate(one_ref[...] + two_ref[...])
    square = (count, count)
    rows = lax.broadcasted_iota(jnp.int32, square, 0)
    lanes = lax.broadcasted_iota(jnp.int32, square, 1)
    factor, coef = work[:, :count], work[:, count:]
    upper[...] = jnp.where(lanes >= rows, factor, 0.0) * jnp.float32(1.0 / root)
    coef_out[...] = coef * jnp.float32(1.0 / root)
    copies = []
    for i, (source, target) in enumerate(((upper, upper_ref), (coef_out, coef_ref))):
        copy = pltpu.make_async_copy(source, target, small_sems.at[i])
        copy.start()
        copies.append(copy)
    inverse = jnp.where(lanes < rows, factor, jnp.where(lanes == rows, scale[:, :count], 0.0))
    weights = outer_sum(coef, inverse)
    high, low = split_bf16(jnp.concatenate([inverse * jnp.float32(root), weights], axis=0))
    left = jnp.concatenate([high, high, low, low], axis=1)
    fetch.wait()
    chunks = out_sems.shape[0]
    width = panel_ref.shape[1] // chunks
    for c in range(chunks):
        here = slice(c * width, (c + 1) * width)
        block = panel_ref[:, here]
        both = jnp.dot(
            left, jnp.concatenate([block, block], axis=0), preferred_element_type=jnp.float32
        )
        basis[:, here] = both[:count]
        left_over[:, here] = trail[:, here] - both[count:]
        for i, (source, target) in enumerate(((basis, basis_ref), (left_over, next_ref))):
            copy = pltpu.make_async_copy(source.at[:, here], target.at[:, here], out_sems.at[c, i])
            copy.start()
            copies.append(copy)
    for copy in copies:
        copy.wait()


def on_device(candidates, trailing, pivots):
    cand_count, width = candidates.shape
    count = pivots.shape[0]
    col_count, row_count = lax.axis_size("col"), lax.axis_size("row")
    x_count = col_count // CORES
    capacity = count // 2
    piece = width // col_count
    root = float(np.sqrt(np.float32(width * row_count)))
    my_col = lax.axis_index("col")
    owners = pivots // cand_count
    order = jnp.arange(count, dtype=jnp.int32)
    earlier = (owners[:, None] == owners[None, :]) & (order[None, :] < order[:, None])
    slots = jnp.sum(earlier.astype(jnp.int32), axis=1)
    away = (owners // CORES) ^ (my_col // CORES)
    keys = jnp.where(owners % CORES == my_col % CORES, away * capacity + slots, -1)[:, None]
    f32 = jnp.float32

    def to_x(array, k, cross):
        return lax.ppermute(array, "col", [(i, i ^ (CORES * k + cross)) for i in range(col_count)])

    def to_core(array):
        return lax.ppermute(array, "col", [(i, i ^ 1) for i in range(col_count)])

    def to_row(array, k):
        return lax.ppermute(array, "row", [(i, i ^ k) for i in range(row_count)])

    def near(array):
        return pltpu.with_memory_space_constraint(array, VMEM)

    in_vmem, in_smem = pl.BlockSpec(memory_space=VMEM), pl.BlockSpec(memory_space=SMEM)
    quarters = pl.pallas_call(
        functools.partial(select_kernel, x_count),
        out_shape=[VMEM((capacity, width // x_count), f32)] * x_count,
        in_specs=[in_smem, pl.BlockSpec(memory_space=pl.ANY)],
        out_specs=[in_vmem] * x_count,
        scratch_shapes=[VMEM((capacity, width), f32), pltpu.SemaphoreType.DMA((capacity,))],
        name="select",
    )(pivots, candidates)
    arrived = [quarters[0]] + [to_x(quarters[k], k, 0) for k in range(1, x_count)]
    keep, send = pl.pallas_call(
        functools.partial(merge_kernel, x_count),
        out_shape=[VMEM((count, piece), f32)] * 2,
        in_specs=[in_vmem] * (1 + x_count),
        out_specs=[in_vmem] * 2,
        name="merge",
    )(near(keys), *map(near, arrived))
    own_piece = keep + to_core(send)
    mine = [own_piece] + [to_x(own_piece, k, 0) for k in range(1, x_count)]
    other = [to_core(array) for array in mine]
    sums, panel = pl.pallas_call(
        functools.partial(gram_kernel, x_count),
        out_shape=[VMEM((count, 2 * count), f32), VMEM((2 * count, width), jnp.bfloat16)],
        in_specs=[in_vmem] * (2 * x_count + 1),
        out_specs=[in_vmem] * 2,
        name="gram",
    )(*map(near, mine), *map(near, other), near(trailing))
    for partners in ((1, 2, 3), (4, 8, 12)):
        terms = [sums] + [to_row(sums, k) for k in partners]
        while len(terms) > 1:
            terms = [one + two for one, two in zip(terms[::2], terms[1::2])]
        sums = terms[0]
    far = to_row(sums, 28)
    anywhere = pl.BlockSpec(memory_space=pl.ANY)
    large = (count, width)
    return pl.pallas_call(
        functools.partial(finish_kernel, root),
        out_shape=[jax.ShapeDtypeStruct((count, count), f32)] * 2
        + [jax.ShapeDtypeStruct(large, f32)] * 2,
        in_specs=[in_vmem] * 3 + [anywhere],
        out_specs=[anywhere] * 4,
        scratch_shapes=[VMEM((count, count), f32)] * 2
        + [VMEM(large, f32)] * 3
        + [pltpu.SemaphoreType.DMA(shape) for shape in ((), (2,), (4, 2))],
        name="finish",
    )(near(sums), near(far), near(panel), trailing)


def solution(mesh):
    placed = (P("col", "row"), P("col", "row"), P())
    return jax.shard_map(
        on_device,
        mesh=mesh,
        in_specs=placed,
        out_specs=(P(), P(None, "col"), P(None, "row"), P("col", "row")),
        check_vma=False,
    )
```

```python
import functools

import jax
import jax.numpy as jnp
import numpy as np
from jax import lax
from jax.experimental import pallas as pl
from jax.experimental.pallas import tpu as pltpu
from jax.sharding import PartitionSpec as P

VMEM = pltpu.VMEM
SMEM = pltpu.SMEM
CORES = 2


def split_bf16(value):
    high = value.astype(jnp.bfloat16)
    low = (value - high.astype(jnp.float32)).astype(jnp.bfloat16)
    return high, low


def select_kernel(x_count, pivots_ref, cand_ref, *rest):
    outs, (rows, sems) = rest[:x_count], rest[x_count:]
    cand_count, width = cand_ref.shape
    count = pivots_ref.shape[0]
    me = lax.axis_index("col")
    first = me * cand_count
    rows[...] = jnp.zeros_like(rows)

    def row_copy(pivot, slot):
        return pltpu.make_async_copy(
            cand_ref.at[pl.ds(pivot - first, 1), :], rows.at[pl.ds(slot, 1), :], sems.at[slot]
        )

    def fetch(i, slot):
        pivot = pivots_ref[i]
        mine = (pivot >= first) & (pivot < first + cand_count)

        @pl.when(mine)
        def _():
            row_copy(pivot, slot).start()

        return slot + mine.astype(jnp.int32)

    total = lax.fori_loop(0, count, fetch, jnp.int32(0), unroll=8)

    def drain(slot, carry):
        row_copy(first, slot).wait()
        return carry

    lax.fori_loop(0, total, drain, 0)
    part = width // x_count
    for k in range(x_count):
        begin = pl.multiple_of(((me // CORES) ^ k) * part, part)
        outs[k][...] = rows[:, pl.ds(begin, part)]


def merge_kernel(x_count, keys_ref, *rest):
    sources, (keep_ref, send_ref) = rest[:x_count], rest[x_count:]
    count, half = keep_ref.shape
    held = x_count * sources[0].shape[0]
    my_core = lax.axis_index("col") % CORES
    lanes = lax.broadcasted_iota(jnp.int32, (count, held), 1)
    pick = (keys_ref[...] == lanes).astype(jnp.float32).astype(jnp.bfloat16)
    pick = jnp.concatenate([pick, pick], axis=1)
    for out_ref, core in ((send_ref, 1 - my_core), (keep_ref, my_core)):
        begin = pl.multiple_of(core * half, half)
        value = jnp.concatenate([ref[:, pl.ds(begin, half)] for ref in sources], axis=0)
        parts = jnp.concatenate(split_bf16(value), axis=0)
        out_ref[...] = jnp.dot(pick, parts, preferred_element_type=jnp.float32)


def gram_kernel(x_count, *rest):
    mine, other = rest[:x_count], rest[x_count : 2 * x_count]
    trail_ref, sums_ref, panel_ref = rest[2 * x_count :]
    count, piece = mine[0].shape
    width = trail_ref.shape[1]
    me = lax.axis_index("col")
    my_x, my_core = me // CORES, me % CORES
    for k in range(x_count):
        near_core = my_core
        for core, ref in ((near_core, mine[k]), (1 - near_core, other[k])):
            begin = pl.multiple_of(((my_x ^ k) * CORES + core) * piece, piece)
            high, low = split_bf16(ref[...])
            panel_ref[0:count, pl.ds(begin, piece)] = high
            panel_ref[count : 2 * count, pl.ds(begin, piece)] = low
    total = jnp.zeros((2 * count, 4 * count), jnp.float32)
    for begin in range(0, width, piece):
        block = slice(begin, begin + piece)
        trail_high, trail_low = split_bf16(trail_ref[:, block])
        panel_parts = panel_ref[:, block]
        right = jnp.concatenate(
            [panel_parts[:count], trail_high, panel_parts[count:], trail_low], axis=0
        )
        total += lax.dot_general(
            panel_parts, right, (((1,), (1,)), ((), ())), preferred_element_type=jnp.float32
        )
    lead = total[:count] + total[count:]
    sums_ref[...] = lead[:, : 2 * count] + lead[:, 2 * count :]


def outer_sum(left, right):
    def parts(value):
        first = value.astype(jnp.bfloat16).astype(jnp.float32)
        rest = value - first
        second = rest.astype(jnp.bfloat16).astype(jnp.float32)
        return first, second, rest - second

    l1, l2, l3 = parts(left)
    r1, r2, r3 = parts(right)
    return lax.dot_general(
        jnp.concatenate([l1, l1, l2, l2, l1, l3], axis=0).astype(jnp.bfloat16),
        jnp.concatenate([r1, r2, r1, r2, r3, r1], axis=0).astype(jnp.bfloat16),
        (((0,), (0,)), ((), ())),
        preferred_element_type=jnp.float32,
    )


def eliminate(work):
    size, group = 32, 8
    count, width = work.shape
    shape = (group, width)
    blocks = [work[begin : begin + group] for begin in range(0, count, group)]
    scales = [jnp.zeros(shape, jnp.float32)] * len(blocks)
    rows = lax.broadcasted_iota(jnp.int32, shape, 0)
    lanes = lax.broadcasted_iota(jnp.int32, shape, 1)
    for begin in range(0, count, size):
        first, last = begin // group, (begin + size) // group
        columns = [
            {
                h: jnp.broadcast_to(blocks[h][:, begin + k : begin + k + 1], shape)
                for h in range(first + k // group, last)
            }
            for k in range(size)
        ]
        for j in range(size):
            g, r = first + j // group, j % group
            pivot = jnp.broadcast_to(columns[j][g][r : r + 1], shape)
            inverse = lax.rsqrt(pivot)
            scales[g] = jnp.where(rows == r, inverse, scales[g])
            below = rows > r
            factors = {h: column * inverse for h, column in columns[j].items()}
            factors[g] = jnp.where(below, factors[g], 0.0)
            for k in range(j + 1, size):
                h, s = first + k // group, k % group
                across = jnp.broadcast_to(columns[j][h][s : s + 1], shape) * inverse
                for h in columns[k]:
                    columns[k][h] -= factors[h] * across
            here = lanes == begin + j
            row = jnp.where(here, 1.0, jnp.broadcast_to(blocks[g][r : r + 1], shape)) * inverse
            for h in range(g, last):
                cleared = jnp.where(here & below if h == g else here, 0.0, blocks[h])
                blocks[h] = cleared - factors[h] * row
        for h in range(first, last):
            blocks[h] *= scales[h]
        if last < len(blocks):
            block = jnp.concatenate(blocks[first:last], axis=0)
            scale = jnp.concatenate(scales[first:last], axis=0)
            place = lax.broadcasted_iota(jnp.int32, block.shape, 1) - begin
            order = lax.broadcasted_iota(jnp.int32, block.shape, 0)
            lower = jnp.where(place < order, block, jnp.where(place == order, scale, 0.0))
            inside = (place >= 0) & (place < size)
            update = outer_sum(block[:, :count], jnp.where(inside, lower, block))
            inside = (lanes >= begin) & (lanes < begin + size)
            for h in range(last, len(blocks)):
                blocks[h] = jnp.where(inside, 0.0, blocks[h]) - update[group * h : group * (h + 1)]
    return jnp.concatenate(blocks, axis=0), jnp.concatenate(scales, axis=0)


def finish_kernel(root, one_ref, two_ref, panel_ref, trail_ref, *rest):
    upper_ref, coef_ref, basis_ref, next_ref = rest[:4]
    upper, coef_out, trail, basis, left_over, in_sem, small_sems, out_sems = rest[4:]
    count = one_ref.shape[0]
    fetch = pltpu.make_async_copy(trail_ref, trail, in_sem)
    fetch.start()
    work, scale = eliminate(one_ref[...] + two_ref[...])
    square = (count, count)
    rows = lax.broadcasted_iota(jnp.int32, square, 0)
    lanes = lax.broadcasted_iota(jnp.int32, square, 1)
    factor, coef = work[:, :count], work[:, count:]
    upper[...] = jnp.where(lanes >= rows, factor, 0.0) * jnp.float32(1.0 / root)
    coef_out[...] = coef * jnp.float32(1.0 / root)
    copies = []
    for i, (source, target) in enumerate(((upper, upper_ref), (coef_out, coef_ref))):
        copy = pltpu.make_async_copy(source, target, small_sems.at[i])
        copy.start()
        copies.append(copy)
    inverse = jnp.where(lanes < rows, factor, jnp.where(lanes == rows, scale[:, :count], 0.0))
    weights = outer_sum(coef, inverse)
    high, low = split_bf16(jnp.concatenate([inverse * jnp.float32(root), weights], axis=0))
    left = jnp.concatenate([high, high, low, low], axis=1)
    fetch.wait()
    chunks = out_sems.shape[0]
    width = panel_ref.shape[1] // chunks
    for c in range(chunks):
        here = slice(c * width, (c + 1) * width)
        block = panel_ref[:, here]
        both = jnp.dot(
            left, jnp.concatenate([block, block], axis=0), preferred_element_type=jnp.float32
        )
        basis[:, here] = both[:count]
        left_over[:, here] = trail[:, here] - both[count:]
        for i, (source, target) in enumerate(((basis, basis_ref), (left_over, next_ref))):
            copy = pltpu.make_async_copy(source.at[:, here], target.at[:, here], out_sems.at[c, i])
            copy.start()
            copies.append(copy)
    for copy in copies:
        copy.wait()


def on_device(candidates, trailing, pivots):
    cand_count, width = candidates.shape
    count = pivots.shape[0]
    col_count, row_count = lax.axis_size("col"), lax.axis_size("row")
    x_count = col_count // CORES
    capacity = count // 2
    piece = width // col_count
    root = float(np.sqrt(np.float32(width * row_count)))
    my_col = lax.axis_index("col")
    owners = pivots // cand_count
    order = jnp.arange(count, dtype=jnp.int32)
    earlier = (owners[:, None] == owners[None, :]) & (order[None, :] < order[:, None])
    slots = jnp.sum(earlier.astype(jnp.int32), axis=1)
    away = (owners // CORES) ^ (my_col // CORES)
    keys = jnp.where(owners % CORES == my_col % CORES, away * capacity + slots, -1)[:, None]
    f32 = jnp.float32

    def to_x(array, k, cross):
        return lax.ppermute(array, "col", [(i, i ^ (CORES * k + cross)) for i in range(col_count)])

    def to_core(array):
        return lax.ppermute(array, "col", [(i, i ^ 1) for i in range(col_count)])

    def to_row(array, k):
        return lax.ppermute(array, "row", [(i, i ^ k) for i in range(row_count)])

    def near(array):
        return pltpu.with_memory_space_constraint(array, VMEM)

    in_vmem, in_smem = pl.BlockSpec(memory_space=VMEM), pl.BlockSpec(memory_space=SMEM)
    quarters = pl.pallas_call(
        functools.partial(select_kernel, x_count),
        out_shape=[VMEM((capacity, width // x_count), f32)] * x_count,
        in_specs=[in_smem, pl.BlockSpec(memory_space=pl.ANY)],
        out_specs=[in_vmem] * x_count,
        scratch_shapes=[VMEM((capacity, width), f32), pltpu.SemaphoreType.DMA((capacity,))],
        name="select",
    )(pivots, candidates)
    arrived = [quarters[0]] + [to_x(quarters[k], k, 0) for k in range(1, x_count)]
    keep, send = pl.pallas_call(
        functools.partial(merge_kernel, x_count),
        out_shape=[VMEM((count, piece), f32)] * 2,
        in_specs=[in_vmem] * (1 + x_count),
        out_specs=[in_vmem] * 2,
        name="merge",
    )(near(keys), *map(near, arrived))
    own_piece = keep + to_core(send)
    mine = [own_piece] + [to_x(own_piece, k, 0) for k in range(1, x_count)]
    other = [to_core(array) for array in mine]
    sums, panel = pl.pallas_call(
        functools.partial(gram_kernel, x_count),
        out_shape=[VMEM((count, 2 * count), f32), VMEM((2 * count, width), jnp.bfloat16)],
        in_specs=[in_vmem] * (2 * x_count + 1),
        out_specs=[in_vmem] * 2,
        name="gram",
    )(*map(near, mine), *map(near, other), near(trailing))
    for partners in ((1, 2, 3), (4, 8, 12)):
        terms = [sums] + [to_row(sums, k) for k in partners]
        while len(terms) > 1:
            terms = [one + two for one, two in zip(terms[::2], terms[1::2])]
        sums = terms[0]
    far = to_row(sums, 28)
    anywhere = pl.BlockSpec(memory_space=pl.ANY)
    large = (count, width)
    return pl.pallas_call(
        functools.partial(finish_kernel, root),
        out_shape=[jax.ShapeDtypeStruct((count, count), f32)] * 2
        + [jax.ShapeDtypeStruct(large, f32)] * 2,
        in_specs=[in_vmem] * 3 + [anywhere],
        out_specs=[anywhere] * 4,
        scratch_shapes=[VMEM((count, count), f32)] * 2
        + [VMEM(large, f32)] * 3
        + [pltpu.SemaphoreType.DMA(shape) for shape in ((), (2,), (4, 2))],
        name="finish",
    )(near(sums), near(far), near(panel), trailing)


def solution(mesh):
    placed = (P("col", "row"), P("col", "row"), P())
    return jax.shard_map(
        on_device,
        mesh=mesh,
        in_specs=placed,
        out_specs=(P(), P(None, "col"), P(None, "row"), P("col", "row")),
        check_vma=False,
    )
```
